32 devices in a mesh: cell: 2 (over x), dom: 16 (over z, y, core).
Axes of the slice: x: 2, y: 2, z: 4, core: 2. Of those that a mesh axis runs over, the one named last changes fastest.
Arguments:
- feats: bfloat16 [2, 2048, 128], P('cell', 'dom'), may hold values from -6 to 6
- positions: float32 [2, 3, 2048], P('cell', None, 'dom'), may hold values from 0 to 1
- species: int32 [2, 2048], P('cell', 'dom'), may hold values from 0 to 7
- wave_vectors: int32 [3, 2048], replicated, may hold values from -8 to 8, as said below
- smearing: float32 [128], replicated, may hold values from 0.001 to 0.03
- species_gain: float32 [8, 128], replicated, may hold values from 0.5 to 1.5
- w_charge: bfloat16 [128, 128], replicated, may hold values from -0.5 to 0.5
- w_message: bfloat16 [128, 128], replicated, may hold values from -0.5 to 0.5
- w_radial: float32 [8, 128], replicated, may hold values from -2 to 2
- w_out: bfloat16 [128, 128], replicated, may hold values from -0.5 to 0.5
- edge_sender: int32 [2, 196608], P('cell', 'dom'), may hold values from 0 to 191
- edge_receiver: int32 [2, 196608], P('cell', 'dom'), may hold values from 0 to 127
- edge_mask: int32 [2, 196608], P('cell', 'dom'), may hold values 0 or 1
- edge_length: float32 [2, 196608], P('cell', 'dom'), may hold values from 0.8 to 5.8
- ghost_down: int32 [2, 512], P('cell', 'dom'), may hold values from 0 to 127
- ghost_up: int32 [2, 512], P('cell', 'dom'), may hold values from 0 to 127
- cotangent: bfloat16 [2, 2048, 128], P('cell', 'dom'), may hold values from -6 to 6
Outputs:
- updated: bfloat16 [2, 2048, 128], P('cell', 'dom')
- feat_grad: bfloat16 [2, 2048, 128], P('cell', 'dom')
- grad_charge: float32 [128, 128], replicated
- grad_message: float32 [128, 128], replicated
- grad_radial: float32 [8, 128], replicated
- grad_out: float32 [128, 128], replicated
The draws below stay inside these ranges and needn't reach their ends.
Inputs may be any that keep to these rules, and one draw needn't show every extreme that they name: `wave_vectors`: every column is a nonzero integer triple. `edge_sender`: rows below 128 are the domain's own atoms, then 32 rows from below, then 32 from above. `edge_receiver`: local row within the domain. `ghost_down`: local row within the sending domain; rows may repeat. `ghost_up`: local row within the sending domain; rows may repeat.
All inputs are finite; a program needn't handle non-finite values. No bound on the sum of `edge_mask` on one device may be relied on, other than what follows from the above.
Results may differ from the reference program's by a relative error of at most 0.01.
Values may be sent and summed in bfloat16 or wider, within the bound.
A program may use at most 64 MiB of HBM per device.

```python
import math
import jax
import jax.numpy as jnp
from jax import lax

C = 128
K = 2048
NB = 8
SPECIES = 8
ATOMS_DEV = 128
GHOST = 32
EDGES_DEV = 12288
ATOMS = 2048
GHOSTS = 512
EDGES = 196608
CELLS = 2
N_DOM = 16


def draw_wave_vectors(key, part):
    key = jax.random.fold_in(key, 11)
    lattice = jax.random.randint(key, (3, K), -8, 9)
    vanish = jnp.all(lattice == 0, axis=0)
    first = jnp.where(vanish, 1, lattice[0])
    return lattice.at[0].set(first).astype(jnp.int32)


def set_ends(values, key, smallest, largest):
    place = [jax.random.randint(jax.random.fold_in(key, axis), (), 0, length) for axis, length in enumerate(values.shape)]
    main_axis = values.shape.index(max(values.shape))
    beside = place[:main_axis] + [(place[main_axis] + 1) % values.shape[main_axis]] + place[main_axis + 1:]
    return values.at[tuple(place)].set(smallest).at[tuple(beside)].set(largest)


def block_levels(own_key, extent, pieces, low, high):
    loudness = 1.0
    for axis_at, parts in pieces:
        draws = jax.random.uniform(jax.random.fold_in(jax.random.fold_in(own_key, 6), axis_at), (parts,), jnp.float32, low / len(pieces), high / len(pieces))
        loudness = loudness * jnp.repeat(jnp.exp(draws), extent[axis_at] // parts).reshape((-1,) + (1,) * (len(extent) - 1 - axis_at))
    return loudness


def scatter_about(own_key, extent, deviation, bound, shards=(), kind=jnp.bfloat16):
    drawn = jax.random.normal(own_key, extent, jnp.float32) * deviation
    if len(shards) > 0:
        drawn = block_levels(own_key, extent, shards, -0.22, 0.18) * drawn
    return jnp.clip(drawn, min=-bound, max=bound).astype(kind)


def setup_inputs(seed: int = 0) -> dict:
    key_of = jax.random.split(jax.random.key(seed), 18)
    return {
        "feats": scatter_about(key_of[0], (CELLS, ATOMS, C), 1.0, 6.0, ((0, 2), (1, 16))),
        "positions": jnp.clip(1.0 * jax.random.uniform(key_of[1], (CELLS, 3, ATOMS), jnp.float32) ** block_levels(key_of[1], (CELLS, 3, ATOMS), ((0, 2), (2, 16)), -0.2, 0.2), 0.0, 1.0),
        "species": set_ends(jax.random.randint(key_of[2], (CELLS, ATOMS), 0, SPECIES), jax.random.fold_in(key_of[2], 1), 0, SPECIES - 1).astype(jnp.int32),
        "wave_vectors": draw_wave_vectors(jax.random.fold_in(key_of[17], 71), 0),
        "smearing": jnp.clip(jnp.exp(jax.random.uniform(key_of[4], (C,), jnp.float32, math.log(0.001), math.log(0.03))), 0.001, 0.03),
        "species_gain": jnp.clip(jax.random.uniform(key_of[5], (SPECIES, C), jnp.float32, 0.5, 1.5), 0.5, 1.5),
        "w_charge": scatter_about(key_of[6], (C, C), C ** -0.5, 0.5),
        "w_message": scatter_about(key_of[7], (C, C), C ** -0.5, 0.5),
        "w_radial": scatter_about(key_of[8], (NB, C), NB ** -0.5, 2.0, (), jnp.float32),
        "w_out": scatter_about(key_of[9], (C, C), C ** -0.5, 0.5),
        "edge_sender": set_ends(jax.random.randint(key_of[10], (CELLS, EDGES), 0, ATOMS_DEV + 2 * GHOST), jax.random.fold_in(key_of[10], 1), 0, (ATOMS_DEV + 2 * GHOST) - 1).astype(jnp.int32),
        "edge_receiver": set_ends(jax.random.randint(key_of[11], (CELLS, EDGES), 0, ATOMS_DEV), jax.random.fold_in(key_of[11], 1), 0, ATOMS_DEV - 1).astype(jnp.int32),
        "edge_mask": set_ends((jax.random.randint(key_of[12], (CELLS, EDGES), 0, 8) < 7).astype(jnp.int32), jax.random.fold_in(key_of[12], 1), 0, 1),
        "edge_length": jnp.clip(0.8 + 5 * jax.random.uniform(key_of[13], (CELLS, EDGES), jnp.float32) ** block_levels(key_of[13], (CELLS, EDGES), ((0, 2), (1, 16)), -0.2, 0.2), 0.8, 5.8),
        "ghost_down": set_ends(jax.random.randint(key_of[14], (CELLS, GHOSTS), 0, ATOMS_DEV), jax.random.fold_in(key_of[14], 1), 0, ATOMS_DEV - 1).astype(jnp.int32),
        "ghost_up": set_ends(jax.random.randint(key_of[15], (CELLS, GHOSTS), 0, ATOMS_DEV), jax.random.fold_in(key_of[15], 1), 0, ATOMS_DEV - 1).astype(jnp.int32),
        "cotangent": scatter_about(key_of[16], (CELLS, ATOMS, C), 1.0, 6.0, ((0, 2), (1, 16))),
    }


cutoff_radius = 6.0
basis_width = 0.75
edge_scale = 0.25
filter_factor = 12.0

def phase_tables(coords, wave_vectors):
    waves = wave_vectors.astype(jnp.float32)
    theta = coords[0][:, None] * waves[0][None, :] + coords[1][:, None] * waves[1][None, :] + coords[2][:, None] * waves[2][None, :]
    theta = 2.0 * math.pi * theta
    return (jnp.cos(theta).astype(jnp.bfloat16), jnp.sin(theta).astype(jnp.bfloat16))

def filter_table(wave_vectors, smearing):
    waves = wave_vectors.astype(jnp.float32)
    squared = lax.optimization_barrier(jnp.sum(waves * waves, axis=0))
    return filter_factor * jnp.exp(-squared[:, None] * smearing[None, :]) / jnp.sqrt(squared)[:, None]

def radial_terms(lengths, w_radial):
    centers = 0.5 + basis_width * jnp.arange(w_radial.shape[0]).astype(jnp.float32)
    basis = jnp.exp(-jnp.square((lengths[:, None] - centers[None, :]) / basis_width))
    envelope = 0.5 * (jnp.cos(math.pi * lengths / cutoff_radius) + 1.0)
    radial = envelope[:, None] * jnp.dot(basis, w_radial, precision=lax.Precision.HIGHEST)
    return (basis, envelope, radial)

def reference(feats, positions, species, wave_vectors, smearing, species_gain, w_charge, w_message, w_radial, w_out, edge_sender, edge_receiver, edge_mask, edge_length, ghost_down, ghost_up, cotangent):
    inv_atoms = 1.0 / math.sqrt(ATOMS)
    inv_waves = 1.0 / math.sqrt(K)
    filt = filter_table(wave_vectors, smearing)

    def take_rows(rows, index):
        return rows[index]

    def one_cell(packed):
        cell_feats, coords, kinds, senders, receivers, masks, lengths, downs, ups, cell_cot = packed
        gain = species_gain[kinds]
        charges = (jnp.dot(cell_feats, w_charge, preferred_element_type=jnp.float32) * gain).astype(jnp.bfloat16)
        coord_blocks = coords.reshape(3, N_DOM, ATOMS_DEV).transpose(1, 0, 2)
        charge_blocks = charges.reshape(N_DOM, ATOMS_DEV, C)

        def structure_block(block):
            coord, values = block
            cos_table, sin_table = phase_tables(coord, wave_vectors)
            return (jnp.dot(cos_table.T, values, preferred_element_type=jnp.float32), jnp.dot(sin_table.T, values, preferred_element_type=jnp.float32))
        parts_re, parts_im = lax.map(structure_block, (coord_blocks, charge_blocks))
        field_re = (filt * lax.optimization_barrier(jnp.sum(parts_re, axis=0)) * inv_atoms).astype(jnp.bfloat16)
        field_im = (filt * lax.optimization_barrier(jnp.sum(parts_im, axis=0)) * inv_atoms).astype(jnp.bfloat16)

        def potential_block(coord):
            cos_table, sin_table = phase_tables(coord, wave_vectors)
            total = jnp.dot(cos_table, field_re, preferred_element_type=jnp.float32) + jnp.dot(sin_table, field_im, preferred_element_type=jnp.float32)
            return total * inv_waves
        potential = lax.map(potential_block, coord_blocks).reshape(ATOMS, C)
        feat_blocks = cell_feats.reshape(N_DOM, ATOMS_DEV, C)
        down_blocks = downs.reshape(N_DOM, GHOST)
        up_blocks = ups.reshape(N_DOM, GHOST)
        sent_down = jax.vmap(take_rows)(feat_blocks, down_blocks)
        sent_up = jax.vmap(take_rows)(feat_blocks, up_blocks)
        from_below = jnp.roll(sent_up, 1, axis=0)
        from_above = jnp.roll(sent_down, -1, axis=0)
        extended = jnp.concatenate([feat_blocks, from_below, from_above], axis=1)
        edge_blocks = (extended, senders.reshape(N_DOM, EDGES_DEV), receivers.reshape(N_DOM, EDGES_DEV), masks.reshape(N_DOM, EDGES_DEV), lengths.reshape(N_DOM, EDGES_DEV))

        def edge_block(block):
            rows, send, recv, live, length = block
            message_rows = jnp.dot(rows, w_message, preferred_element_type=jnp.float32).astype(jnp.bfloat16)
            basis, envelope, radial = radial_terms(length, w_radial)
            picked = message_rows[send].astype(jnp.float32)
            messages = live.astype(jnp.float32)[:, None] * radial * picked
            return jnp.zeros((ATOMS_DEV, C), jnp.float32).at[recv].add(messages) * edge_scale
        aggregate = lax.map(edge_block, edge_blocks).reshape(ATOMS, C)
        preact = aggregate + potential
        act = jax.nn.silu(preact).astype(jnp.bfloat16)
        updated = (cell_feats.astype(jnp.float32) + jnp.dot(act, w_out, preferred_element_type=jnp.float32)).astype(jnp.bfloat16)
        grad_act = jnp.dot(cell_cot, w_out.T, preferred_element_type=jnp.float32)
        sig = jax.nn.sigmoid(preact)
        grad_pre = grad_act * sig * (1.0 + preact * (1.0 - sig))
        grad_pre_b = grad_pre.astype(jnp.bfloat16)
        grad_out = jnp.dot(act.T, cell_cot, preferred_element_type=jnp.float32)
        back_re, back_im = lax.map(structure_block, (coord_blocks, grad_pre_b.reshape(N_DOM, ATOMS_DEV, C)))
        dfield_re = (filt * lax.optimization_barrier(jnp.sum(back_re, axis=0)) * (inv_waves * inv_atoms)).astype(jnp.bfloat16)
        dfield_im = (filt * lax.optimization_barrier(jnp.sum(back_im, axis=0)) * (inv_waves * inv_atoms)).astype(jnp.bfloat16)

        def charge_block(coord):
            cos_table, sin_table = phase_tables(coord, wave_vectors)
            return jnp.dot(cos_table, dfield_re, preferred_element_type=jnp.float32) + jnp.dot(sin_table, dfield_im, preferred_element_type=jnp.float32)
        grad_charges = lax.map(charge_block, coord_blocks).reshape(ATOMS, C)
        grad_raw = (grad_charges * gain).astype(jnp.bfloat16)
        grad_charge = jnp.dot(cell_feats.T, grad_raw, preferred_element_type=jnp.float32)
        feat_from_charge = jnp.dot(grad_raw, w_charge.T, preferred_element_type=jnp.float32)

        def edge_back(block):
            rows, send, recv, live, length, upper = block
            message_rows = jnp.dot(rows, w_message, preferred_element_type=jnp.float32).astype(jnp.bfloat16)
            basis, envelope, radial = radial_terms(length, w_radial)
            picked = message_rows[send].astype(jnp.float32)
            livef = live.astype(jnp.float32)[:, None]
            upstream = upper[recv] * edge_scale
            grad_picked = livef * radial * upstream
            grad_radial_edge = livef * picked * upstream
            grad_msg = jnp.zeros((ATOMS_DEV + 2 * GHOST, C), jnp.float32).at[send].add(grad_picked).astype(jnp.bfloat16)
            part_message = jnp.dot(rows.T, grad_msg, preferred_element_type=jnp.float32)
            grad_rows = jnp.dot(grad_msg, w_message.T, preferred_element_type=jnp.float32)
            part_radial = jnp.dot(basis.T, envelope[:, None] * grad_radial_edge, precision=lax.Precision.HIGHEST)
            return (grad_rows, part_message, part_radial)
        grad_rows, parts_message, parts_radial = lax.map(edge_back, edge_blocks + (grad_pre.reshape(N_DOM, ATOMS_DEV, C),))
        back_below = grad_rows[:, ATOMS_DEV:ATOMS_DEV + GHOST]
        back_above = grad_rows[:, ATOMS_DEV + GHOST:]
        to_down = jnp.roll(back_above, 1, axis=0)
        to_up = jnp.roll(back_below, -1, axis=0)
        own_total = (cell_cot.astype(jnp.float32) + feat_from_charge).reshape(N_DOM, ATOMS_DEV, C) + grad_rows[:, :ATOMS_DEV]

        def add_back(total, down_index, up_index, down_rows, up_rows):
            return total.at[down_index].add(down_rows).at[up_index].add(up_rows)
        own_total = jax.vmap(add_back)(own_total, down_blocks, up_blocks, to_down, to_up)
        feat_grad = own_total.reshape(ATOMS, C).astype(jnp.bfloat16)
        return (updated, feat_grad, grad_charge, lax.optimization_barrier(jnp.sum(parts_message, axis=0)), lax.optimization_barrier(jnp.sum(parts_radial, axis=0)), grad_out)
    results = lax.map(one_cell, (feats, positions, species, edge_sender, edge_receiver, edge_mask, edge_length, ghost_down, ghost_up, cotangent))
    scale = 1.0 / math.sqrt(CELLS * ATOMS)
    return (results[0], results[1], lax.optimization_barrier(jnp.sum(results[2], axis=0)) * scale, lax.optimization_barrier(jnp.sum(results[3], axis=0)) * scale, lax.optimization_barrier(jnp.sum(results[4], axis=0)) * scale, lax.optimization_barrier(jnp.sum(results[5], axis=0)) * scale)
```

```python
import math

import jax
import jax.numpy as jnp
from jax import lax
from jax.experimental import pallas as pl
from jax.experimental.pallas import tpu as pltpu
from jax.sharding import PartitionSpec as P

cutoff_radius = 6.0
basis_width = 0.75
edge_scale = 0.25
filter_factor = 12.0


def extended_2(block, sides, width):
    for axis, dim in sides:
        count = lax.axis_size(axis)
        forward = [(i, i + 1) for i in range(count - 1)]
        forward.append((count - 1, 0))
        backward = [(target, source) for source, target in forward]
        low = lax.ppermute(
            lax.slice_in_dim(block, block.shape[dim] - width, None, axis=dim), axis, forward
        )
        high = lax.ppermute(lax.slice_in_dim(block, 0, width, axis=dim), axis, backward)
        block = jnp.concatenate([low, block, high], axis=dim)
    return block


def phase_tables(coords, wave_vectors):
    waves = wave_vectors.astype(jnp.float32)
    theta = (
        coords[0][:, None] * waves[0][None, :]
        + coords[1][:, None] * waves[1][None, :]
        + coords[2][:, None] * waves[2][None, :]
    )
    theta = 2.0 * math.pi * theta
    return (jnp.cos(theta).astype(jnp.bfloat16), jnp.sin(theta).astype(jnp.bfloat16))


def filter_table(wave_vectors, smearing):
    waves = wave_vectors.astype(jnp.float32)
    squared = jnp.sum(waves * waves, axis=0)
    return (
        filter_factor * jnp.exp(-squared[:, None] * smearing[None, :]) / jnp.sqrt(squared)[:, None]
    )


def contract_rows(left, right):
    return lax.dot_general(
        left, right, (((0,), (0,)), ((), ())), preferred_element_type=jnp.float32
    )


def reduced_field(local_re, local_im, filt, scale):
    total_re, total_im = lax.psum((local_re, local_im), "dom")
    return (
        (filt * total_re * scale).astype(jnp.bfloat16),
        (filt * total_im * scale).astype(jnp.bfloat16),
    )


def pair_weights_kernel(senders, receivers, mask, lengths, out_ref, total, *, chunk, bases):
    atoms = out_ref.shape[0] // bases
    rows = out_ref.shape[1]
    total[...] = jnp.zeros_like(total)

    def body(step, carry):
        at = pl.ds(pl.multiple_of(step * chunk, chunk), chunk)
        length = lengths[:, at]
        centers = 0.5 + basis_width * lax.broadcasted_iota(jnp.int32, (bases, chunk), 0).astype(
            jnp.float32
        )
        basis = jnp.exp(-jnp.square((length - centers) / basis_width))
        turn = math.pi * (length / cutoff_radius - 0.5)
        square = turn * turn
        sine = jnp.float32(-1.0 / 39916800.0)
        for factor in (1.0 / 362880.0, -1.0 / 5040.0, 1.0 / 120.0, -1.0 / 6.0, 1.0):
            sine = sine * square + factor
        envelope = 0.5 * (1.0 - turn * sine) * mask[:, at].astype(jnp.float32)
        weights = (basis * envelope).astype(jnp.bfloat16)
        receiver = lax.broadcasted_iota(jnp.int32, (atoms, chunk), 0) == receivers[:, at]
        sender = lax.broadcasted_iota(jnp.int32, (rows, chunk), 0) == senders[:, at]
        receiver = receiver.astype(jnp.bfloat16)
        sender = sender.astype(jnp.bfloat16)
        left = jnp.concatenate([receiver * weights[b : b + 1] for b in range(bases)], axis=0)
        total[...] += lax.dot_general(
            left, sender, (((1,), (1,)), ((), ())), preferred_element_type=jnp.float32
        )
        return carry

    lax.fori_loop(0, lengths.shape[1] // chunk, body, 0)
    out_ref[...] = total[...].astype(out_ref.dtype)


def pair_weights(senders, receivers, mask, lengths, atoms, rows, bases):
    edges = lengths.shape[1]
    shape = (bases * atoms, rows)
    vmem = pl.BlockSpec(memory_space=pltpu.VMEM)
    return pl.pallas_call(
        lambda *refs: pair_weights_kernel(*refs, chunk=1024, bases=bases),
        out_shape=jax.ShapeDtypeStruct(shape, jnp.bfloat16),
        in_specs=[vmem] * 4,
        out_specs=vmem,
        scratch_shapes=[pltpu.VMEM(shape, jnp.float32)],
        compiler_params=pltpu.CompilerParams(vmem_limit_bytes=48 * 1024 * 1024),
        cost_estimate=pl.CostEstimate(
            flops=2 * edges * shape[0] * rows, bytes_accessed=20 * edges, transcendentals=0
        ),
    )(senders, receivers, mask, lengths)


def per_device(
    feats,
    positions,
    species,
    wave_vectors,
    smearing,
    species_gain,
    w_charge,
    w_message,
    w_radial,
    w_out,
    edge_sender,
    edge_receiver,
    edge_mask,
    edge_length,
    ghost_down,
    ghost_up,
    cotangent,
):
    own_rows = feats[0]
    coords = positions[0]
    downs = ghost_down[0]
    ups = ghost_up[0]
    upstream_cot = cotangent[0]
    atoms = own_rows.shape[0]
    ghosts = downs.shape[0]
    domains = lax.axis_size("dom")
    cells = lax.axis_size("cell")
    inv_waves = 1.0 / math.sqrt(wave_vectors.shape[1])
    inv_atoms = 1.0 / math.sqrt(atoms * domains)
    grad_scale = 1.0 / math.sqrt(cells * atoms * domains)
    labels = jnp.arange(species_gain.shape[0], dtype=jnp.int32)
    onehot = (species[0][:, None] == labels[None, :]).astype(jnp.float32)
    gain = jnp.dot(onehot, species_gain, precision=lax.Precision.HIGHEST)
    charges = (jnp.dot(own_rows, w_charge, preferred_element_type=jnp.float32) * gain).astype(
        jnp.bfloat16
    )
    outgoing = jnp.concatenate([own_rows[downs], own_rows[ups]], axis=0)
    padded = extended_2(outgoing, (("dom", 0),), ghosts)
    extended = jnp.concatenate([own_rows, padded[:ghosts], padded[3 * ghosts :]], axis=0)
    cos_table, sin_table = phase_tables(coords, wave_vectors)
    filt = filter_table(wave_vectors, smearing)
    field_re, field_im = reduced_field(
        contract_rows(cos_table, charges), contract_rows(sin_table, charges), filt, inv_atoms
    )
    potential = (
        jnp.dot(cos_table, field_re, preferred_element_type=jnp.float32)
        + jnp.dot(sin_table, field_im, preferred_element_type=jnp.float32)
    ) * inv_waves
    message_rows = jnp.dot(extended, w_message, preferred_element_type=jnp.float32).astype(
        jnp.bfloat16
    )
    bases = w_radial.shape[0]
    pairs = pair_weights(
        edge_sender, edge_receiver, edge_mask, edge_length, atoms, message_rows.shape[0], bases
    )
    mixed = jnp.dot(pairs, message_rows, preferred_element_type=jnp.float32)
    mixed = mixed.reshape(bases, atoms, -1)
    aggregate = jnp.sum(w_radial[:, None, :] * mixed, axis=0) * edge_scale
    preact = aggregate + potential
    act = jax.nn.silu(preact).astype(jnp.bfloat16)
    updated = (
        own_rows.astype(jnp.float32) + jnp.dot(act, w_out, preferred_element_type=jnp.float32)
    ).astype(jnp.bfloat16)
    grad_act = jnp.dot(upstream_cot, w_out.T, preferred_element_type=jnp.float32)
    sig = jax.nn.sigmoid(preact)
    grad_pre = grad_act * sig * (1.0 + preact * (1.0 - sig))
    grad_pre_b = grad_pre.astype(jnp.bfloat16)
    grad_out = contract_rows(act, upstream_cot)
    dfield_re, dfield_im = reduced_field(
        contract_rows(cos_table, grad_pre_b),
        contract_rows(sin_table, grad_pre_b),
        filt,
        inv_waves * inv_atoms,
    )
    grad_charges = jnp.dot(cos_table, dfield_re, preferred_element_type=jnp.float32) + jnp.dot(
        sin_table, dfield_im, preferred_element_type=jnp.float32
    )
    grad_raw = (grad_charges * gain).astype(jnp.bfloat16)
    grad_charge = contract_rows(own_rows, grad_raw)
    feat_from_charge = jnp.dot(grad_raw, w_charge.T, preferred_element_type=jnp.float32)
    weighted = (w_radial[:, None, :] * (edge_scale * grad_pre)[None]).astype(jnp.bfloat16)
    grad_msg = contract_rows(pairs, weighted.reshape(bases * atoms, -1)).astype(jnp.bfloat16)
    grad_message = contract_rows(extended, grad_msg)
    grad_rows = jnp.dot(grad_msg, w_message.T, preferred_element_type=jnp.float32)
    grad_radial = jnp.sum(mixed * (edge_scale * grad_pre)[None], axis=1)
    returning = grad_rows[atoms:]
    padded_back = extended_2(returning, (("dom", 0),), ghosts)
    own_total = upstream_cot.astype(jnp.float32) + feat_from_charge + grad_rows[:atoms]
    own_total = own_total.at[downs].add(padded_back[:ghosts]).at[ups].add(padded_back[3 * ghosts :])
    feat_grad = own_total.astype(jnp.bfloat16)
    partials = (grad_charge, grad_message, grad_radial, grad_out)
    totals = lax.psum((partials[0], partials[1], partials[2], partials[3]), ("cell", "dom"))
    return (
        updated[None],
        feat_grad[None],
        totals[0] * grad_scale,
        totals[1] * grad_scale,
        totals[2] * grad_scale,
        totals[3] * grad_scale,
    )


def solution(mesh):
    placed = (
        P("cell", "dom", None),
        P("cell", None, "dom"),
        P("cell", "dom"),
        P(),
        P(),
        P(),
        P(),
        P(),
        P(),
        P(),
        P("cell", "dom"),
        P("cell", "dom"),
        P("cell", "dom"),
        P("cell", "dom"),
        P("cell", "dom"),
        P("cell", "dom"),
        P("cell", "dom", None),
    )
    return jax.shard_map(
        per_device,
        mesh=mesh,
        in_specs=placed,
        out_specs=(P("cell", "dom", None), P("cell", "dom", None), P(), P(), P(), P()),
        check_vma=False,
    )
```

```python
import functools
import math

import jax
import jax.numpy as jnp
from jax import lax
from jax.experimental import pallas as pl
from jax.experimental.pallas import tpu as pltpu
from jax.sharding import PartitionSpec as P

cutoff_radius = 6.0
basis_width = 0.75
edge_scale = 0.25
filter_factor = 12.0
MESH = pl.DeviceIdType.MESH
edge_chunk = 1024
wave_chunk = 128
lane = 128
part_rows = 8

sine_terms = (32.78140079, -74.47800454, 81.36681529, -41.33121431, 6.2830558)
cosine_terms = (-21.07678176, 58.79403849, -85.27239696, 64.92872661, -19.73898252, 0.99999922)


def horner(terms, x):
    value = terms[0] * x + terms[1]
    for term in terms[2:]:
        value = value * x + term
    return value


def dot(left, right, dims, precision=None):
    return lax.dot_general(
        left, right, (dims, ((), ())), preferred_element_type=jnp.float32, precision=precision
    )


def rows_by_rows(left, right):
    return dot(left, right, ((0,), (0,)))


def plain(left, right):
    return dot(left, right, ((1,), (0,)))


def by_transpose(left, right):
    return dot(left, right, ((1,), (1,)))


def edge_weights(length, mask, bases):
    shape = (bases, length.shape[1])
    centers = 0.5 + basis_width * lax.broadcasted_iota(jnp.int32, shape, 0).astype(jnp.float32)
    basis = jnp.exp(-jnp.square((length - centers) / basis_width))
    turn = math.pi * (length / cutoff_radius - 0.5)
    square = turn * turn
    sine = turn * horner(
        (-1.0 / 39916800.0, 1.0 / 362880.0, -1.0 / 5040.0, 1.0 / 120.0, -1.0 / 6.0, 1.0), square
    )
    return (basis * (0.5 * (1.0 - sine) * mask.astype(jnp.float32))).astype(jnp.bfloat16)


def spread(index, rows):
    shape = (rows, index.shape[1])
    return lax.broadcasted_iota(jnp.int32, shape, 0) == index


def block_kernel(
    domains,
    cells,
    feats,
    positions,
    species,
    waves,
    smearing,
    species_gain,
    w_charge,
    w_message,
    w_radial,
    w_out,
    senders,
    receivers,
    mask,
    lengths,
    ghost_down,
    ghost_up,
    cotangent,
    updated_ref,
    feat_grad_ref,
    grad_charge_ref,
    grad_message_ref,
    grad_radial_ref,
    grad_out_ref,
    pos_all,
    charge_all,
    grad_all,
    outgoing,
    extended,
    returning,
    returned,
    pair_total,
    pairs,
    points,
    wave_rows,
    table,
    own_table,
    field,
    half_out,
    half_in,
    sums_a,
    sums_b,
    slots_a,
    slots_b,
    reduced_a,
    reduced_b,
    owned_a,
    owned_b,
    gather_send,
    gather_recv,
    pass_send,
    pass_recv,
    side_send,
    side_recv,
    half_send,
    half_recv,
    weight_send,
    weight_recv,
):
    atoms = feats.shape[1]
    ghosts = ghost_down.shape[1]
    bases = w_radial.shape[0]
    wave_count = waves.shape[1]
    half = wave_count // 2
    chips = domains // 2
    devices = domains * cells
    inv_waves = 1.0 / math.sqrt(wave_count)
    inv_atoms = 1.0 / math.sqrt(atoms * domains)
    grad_scale = 1.0 / math.sqrt(cells * atoms * domains)

    cell = lax.axis_index("cell")
    me = lax.axis_index("dom")
    core = lax.rem(me, 2)
    chip = lax.div(me, 2)
    partner = me + 1 - 2 * core
    linear = cell * domains + me

    def place(index):
        return (lax.div(index, domains), lax.rem(index, domains))

    barrier = pltpu.get_barrier_semaphore()

    def greet(step, carry):
        target = lax.rem(linear + step, devices)
        pl.semaphore_signal(barrier, inc=1, device_id=place(target), device_id_type=MESH)
        return carry

    lax.fori_loop(1, devices, greet, 0)

    def remote(source, target, send, recv, index):
        return pltpu.make_async_remote_copy(
            src_ref=source,
            dst_ref=target,
            send_sem=send,
            recv_sem=recv,
            device_id=(cell, index),
            device_id_type=MESH,
        )

    rows = feats[0]
    upstream_cot = cotangent[0]
    pos_all[me] = jnp.zeros(pos_all.shape[1:], jnp.float32)
    pos_all[me, 0:3, :] = positions[0]
    kinds = spread(species[...], species_gain.shape[0]).astype(jnp.float32)
    gain = dot(kinds, species_gain[...], ((0,), (0,)), lax.Precision.HIGHEST)
    charge_all[me] = (plain(rows, w_charge[...]) * gain).astype(jnp.bfloat16)
    down_spread = spread(ghost_down[...], atoms).astype(jnp.bfloat16)
    up_spread = spread(ghost_up[...], atoms).astype(jnp.bfloat16)
    outgoing[0] = rows_by_rows(up_spread, rows).astype(jnp.bfloat16)
    outgoing[1] = rows_by_rows(down_spread, rows).astype(jnp.bfloat16)
    extended[0:atoms, :] = rows

    pl.semaphore_wait(barrier, devices - 1)

    def gather_copy(buffer, which, step, index):
        return remote(
            buffer.at[index],
            buffer.at[index],
            gather_send.at[which, step],
            gather_recv.at[which, step],
            lax.rem(chip + step, chips) * 2 + core,
        )

    def pass_copy(buffer, which, step, index):
        return remote(
            buffer.at[index],
            buffer.at[index],
            pass_send.at[which, step],
            pass_recv.at[which, step],
            partner,
        )

    def gather_start(buffer, which):
        pass_copy(buffer, which, 0, me).start()
        for step in range(1, chips):
            gather_copy(buffer, which, step, me).start()

    def gather_finish(buffer, which):
        for step in range(1, chips):
            source = lax.rem(chip - step + chips, chips) * 2 + core
            gather_copy(buffer, which, step, source).wait_recv()
            pass_copy(buffer, which, step, source).start()
        for step in range(chips):
            source = lax.rem(chip - step + chips, chips) * 2 + (1 - core)
            pass_copy(buffer, which, step, source).wait_recv()
        for step in range(1, chips):
            gather_copy(buffer, which, step, me).wait_send()
        for step in range(chips):
            pass_copy(buffer, which, step, me).wait_send()

    gather_start(pos_all, 0)
    gather_start(charge_all, 1)
    above = lax.rem(me + 1, domains)
    below = lax.rem(me + domains - 1, domains)
    low = pl.ds(atoms, ghosts)
    high = pl.ds(atoms + ghosts, ghosts)
    ghost_copies = [
        remote(outgoing.at[0], extended.at[low], side_send.at[0], side_recv.at[0], above),
        remote(outgoing.at[1], extended.at[high], side_send.at[1], side_recv.at[1], below),
    ]
    for copy in ghost_copies:
        copy.start()

    pair_total[...] = jnp.zeros_like(pair_total)

    def edge_step(step, carry):
        at = pl.ds(pl.multiple_of(step * edge_chunk, edge_chunk), edge_chunk)
        weights = edge_weights(lengths[:, at], mask[:, at], bases)
        receiver = spread(receivers[:, at], atoms).astype(jnp.bfloat16)
        sender = spread(senders[:, at], atoms + 2 * ghosts).astype(jnp.bfloat16)
        left = jnp.concatenate([receiver * weights[b : b + 1] for b in range(bases)], axis=0)
        pair_total[...] += by_transpose(left, sender)
        return carry

    lax.fori_loop(0, lengths.shape[1] // edge_chunk, edge_step, 0)
    pairs[...] = pair_total[...].astype(jnp.bfloat16)

    gather_finish(pos_all, 0)
    for index in range(domains):
        place_at = slice(index * atoms, (index + 1) * atoms)
        exact = pos_all[index]
        first = exact.astype(jnp.bfloat16)
        rest = exact - first.astype(jnp.float32)
        second = rest.astype(jnp.bfloat16)
        third = (rest - second.astype(jnp.float32)).astype(jnp.bfloat16)
        points[:, place_at] = jnp.concatenate(
            [first.astype(jnp.float32), second.astype(jnp.float32), third.astype(jnp.float32)],
            axis=0,
        ).astype(jnp.bfloat16)
    wave_rows[...] = jnp.zeros_like(wave_rows)
    wave_rows[0:3, :] = waves[
        :, pl.ds(pl.multiple_of(core * half, wave_chunk), half)
    ].astype(jnp.float32)
    pair_base = pl.multiple_of(chip * 2 * atoms, lane)
    gather_finish(charge_all, 1)
    charges = charge_all[...].reshape(domains * atoms, -1)
    ones = jnp.ones((part_rows, lane), jnp.bfloat16)

    def filter_of(at):
        wave = wave_rows[:, at]
        squared = rows_by_rows((wave * wave).astype(jnp.bfloat16), ones)
        return filter_factor * jnp.exp(-squared * smearing[...]) * lax.rsqrt(squared)

    def table_step(step, carry):
        at = pl.ds(pl.multiple_of(step * wave_chunk, wave_chunk), wave_chunk)
        then = pl.ds(pl.multiple_of(half + step * wave_chunk, wave_chunk), wave_chunk)
        wave = wave_rows[:, at]
        wave = jnp.concatenate([wave, wave, wave], axis=0).astype(jnp.bfloat16)
        turns = rows_by_rows(wave, points[...])
        turns = turns - jnp.floor(turns + 0.5)
        square = turns * turns
        cosine = horner(cosine_terms, square).astype(jnp.bfloat16)
        sine = (turns * horner(sine_terms, square)).astype(jnp.bfloat16)
        table[at, :] = cosine
        table[then, :] = sine
        scaled = filter_of(at) * inv_atoms
        field[at, :] = (scaled * plain(cosine, charges)).astype(jnp.bfloat16)
        field[then, :] = (scaled * plain(sine, charges)).astype(jnp.bfloat16)
        return carry

    lax.fori_loop(0, half // wave_chunk, table_step, 0)
    own_table[...] = table[:, pl.ds(pair_base, 2 * atoms)].T

    def exchange(which):
        partial = plain(own_table[...], field[...])
        half_out[which] = partial.reshape(2, atoms, -1)
        copy = remote(
            half_out.at[which, 1 - core],
            half_in.at[which],
            half_send.at[which],
            half_recv.at[which],
            partner,
        )
        copy.start()
        return copy

    first_exchange = exchange(0)
    for copy in ghost_copies:
        copy.wait()
    message_rows = plain(extended[...], w_message[...]).astype(jnp.bfloat16)
    mixed = plain(pairs[...], message_rows).reshape(bases, atoms, -1)
    aggregate = jnp.zeros((atoms, rows.shape[1]), jnp.float32)
    for b in range(bases):
        aggregate += w_radial[b : b + 1, :] * mixed[b]
    grad_act = by_transpose(upstream_cot, w_out[...])
    first_exchange.wait()
    potential = (half_out[0, core] + half_in[0]) * inv_waves
    preact = aggregate * edge_scale + potential
    sig = 1.0 / (1.0 + jnp.exp(-preact))
    grad_pre = grad_act * sig * (1.0 + preact * (1.0 - sig))
    grad_all[me] = grad_pre.astype(jnp.bfloat16)
    gather_start(grad_all, 2)

    act = (preact * sig).astype(jnp.bfloat16)
    updated_ref[0] = (rows.astype(jnp.float32) + plain(act, w_out[...])).astype(jnp.bfloat16)
    scaled_pre = edge_scale * grad_pre
    weighted = jnp.concatenate(
        [(w_radial[b : b + 1, :] * scaled_pre).astype(jnp.bfloat16) for b in range(bases)], axis=0
    )
    grad_msg = rows_by_rows(pairs[...], weighted).astype(jnp.bfloat16)
    grad_rows = by_transpose(grad_msg, w_message[...])
    returning[...] = grad_rows[atoms:].reshape(returning.shape)
    return_copies = [
        remote(returning.at[0], returned.at[0], side_send.at[2], side_recv.at[2], below),
        remote(returning.at[1], returned.at[1], side_send.at[3], side_recv.at[3], above),
    ]
    for copy in return_copies:
        copy.start()
    sums_a[0:atoms_of(sums_a), :] = rows_by_rows(extended[...], grad_msg)
    sums_a[atoms_of(sums_a) :, :] = rows_by_rows(act, upstream_cot)

    def scatter_start(sums, slots, which):
        owners = sums.shape[0] // part_rows
        slots[linear] = jnp.zeros(slots.shape[1:], jnp.float32)

        def send(step, carry):
            target = lax.rem(linear + step, devices)

            @pl.when(target < owners)
            def _():
                pltpu.make_async_remote_copy(
                    src_ref=sums.at[pl.ds(pl.multiple_of(target * part_rows, part_rows), part_rows)],
                    dst_ref=slots.at[linear],
                    send_sem=weight_send.at[which],
                    recv_sem=weight_recv.at[which],
                    device_id=place(target),
                    device_id_type=MESH,
                ).start()

            return carry

        lax.fori_loop(1, devices, send, 0)

    def wait_bytes(ref, send, recv):
        return pltpu.make_async_remote_copy(
            src_ref=ref,
            dst_ref=ref,
            send_sem=send,
            recv_sem=recv,
            device_id=(cell, partner),
            device_id_type=MESH,
        )

    def scatter_finish(sums, slots, owned, reduced, which):
        owners = sums.shape[0] // part_rows
        mine = pl.ds(pl.multiple_of(lax.rem(linear, owners) * part_rows, part_rows), part_rows)
        send, recv = weight_send.at[which], weight_recv.at[which]

        @pl.when(linear < owners)
        def _():
            wait_bytes(slots.at[pl.ds(0, devices - 1)], send, recv).wait_recv()
            wait_bytes(sums.at[pl.ds(0, (owners - 1) * part_rows)], send, recv).wait_send()
            total = sums[mine, :]
            for index in range(devices):
                total += slots[index]
            owned[...] = total * grad_scale
            reduced[mine, :] = owned[...]

        @pl.when(linear >= owners)
        def _():
            wait_bytes(sums, send, recv).wait_send()

    def share_start(owned, reduced, which):
        owners = reduced.shape[0] // part_rows

        @pl.when(linear < owners)
        def _():
            def send(step, carry):
                target = lax.rem(linear + step, devices)
                pltpu.make_async_remote_copy(
                    src_ref=owned,
                    dst_ref=reduced.at[
                        pl.ds(
                            pl.multiple_of(lax.rem(linear, owners) * part_rows, part_rows),
                            part_rows,
                        )
                    ],
                    send_sem=weight_send.at[which + 1],
                    recv_sem=weight_recv.at[which + 1],
                    device_id=place(target),
                    device_id_type=MESH,
                ).start()
                return carry

            lax.fori_loop(1, devices, send, 0)

    def share_finish(slots, reduced, which):
        owners = reduced.shape[0] // part_rows
        send, recv = weight_send.at[which + 1], weight_recv.at[which + 1]

        @pl.when(linear < owners)
        def _():
            wait_bytes(reduced.at[pl.ds(0, (owners - 1) * part_rows)], send, recv).wait_recv()
            wait_bytes(slots.at[pl.ds(0, devices - 1)], send, recv).wait_send()

        @pl.when(linear >= owners)
        def _():
            wait_bytes(reduced, send, recv).wait_recv()

    scatter_start(sums_a, slots_a, 0)

    grad_radial = jnp.concatenate(
        [jnp.sum(mixed[b] * scaled_pre, axis=0, keepdims=True) for b in range(bases)], axis=0
    )
    sums_b[pl.ds(sums_b.shape[0] - bases, bases), :] = grad_radial

    gather_finish(grad_all, 2)
    grads = grad_all[...].reshape(domains * atoms, -1)

    def back_step(step, carry):
        at = pl.ds(pl.multiple_of(step * wave_chunk, wave_chunk), wave_chunk)
        then = pl.ds(pl.multiple_of(half + step * wave_chunk, wave_chunk), wave_chunk)
        scaled = filter_of(at) * (inv_waves * inv_atoms)
        field[at, :] = (scaled * plain(table[at, :], grads)).astype(jnp.bfloat16)
        field[then, :] = (scaled * plain(table[then, :], grads)).astype(jnp.bfloat16)
        return carry

    lax.fori_loop(0, half // wave_chunk, back_step, 0)
    second_exchange = exchange(1)

    scatter_finish(sums_a, slots_a, owned_a, reduced_a, 0)
    share_start(owned_a, reduced_a, 0)

    second_exchange.wait()
    grad_raw = ((half_out[1, core] + half_in[1]) * gain).astype(jnp.bfloat16)
    sums_b[0 : sums_b.shape[0] - bases, :] = rows_by_rows(rows, grad_raw)
    scatter_start(sums_b, slots_b, 2)
    for copy in return_copies:
        copy.wait()
    total = (
        upstream_cot.astype(jnp.float32)
        + by_transpose(grad_raw, w_charge[...])
        + grad_rows[:atoms]
        + dot(down_spread.astype(jnp.float32), returned[1], ((1,), (0,)), lax.Precision.HIGHEST)
        + dot(up_spread.astype(jnp.float32), returned[0], ((1,), (0,)), lax.Precision.HIGHEST)
    )
    feat_grad_ref[0] = total.astype(jnp.bfloat16)

    scatter_finish(sums_b, slots_b, owned_b, reduced_b, 2)
    share_start(owned_b, reduced_b, 2)
    share_finish(slots_a, reduced_a, 0)
    grad_message_ref[...] = reduced_a[0 : atoms_of(sums_a), :]
    grad_out_ref[...] = reduced_a[atoms_of(sums_a) :, :]
    share_finish(slots_b, reduced_b, 2)
    grad_charge_ref[...] = reduced_b[0 : sums_b.shape[0] - bases, :]
    grad_radial_ref[...] = reduced_b[sums_b.shape[0] - bases :, :]


def atoms_of(sums):
    return sums.shape[0] // 2


def per_device(
    feats,
    positions,
    species,
    wave_vectors,
    smearing,
    species_gain,
    w_charge,
    w_message,
    w_radial,
    w_out,
    edge_sender,
    edge_receiver,
    edge_mask,
    edge_length,
    ghost_down,
    ghost_up,
    cotangent,
):
    domains = lax.axis_size("dom")
    cells = lax.axis_size("cell")
    atoms, width = feats.shape[1:]
    ghosts = ghost_down.shape[1]
    bases = w_radial.shape[0]
    wave_count = wave_vectors.shape[1]
    devices = domains * cells
    chips = domains // 2
    f32, bf16 = jnp.float32, jnp.bfloat16
    vmem = pl.BlockSpec(memory_space=pltpu.VMEM)
    count_a = 2 * width
    count_b = width + bases
    scratch = [
        pltpu.VMEM((domains, part_rows, atoms), f32),
        pltpu.VMEM((domains, atoms, width), bf16),
        pltpu.VMEM((domains, atoms, width), bf16),
        pltpu.VMEM((2, ghosts, width), bf16),
        pltpu.VMEM((atoms + 2 * ghosts, width), bf16),
        pltpu.VMEM((2, ghosts, width), f32),
        pltpu.VMEM((2, ghosts, width), f32),
        pltpu.VMEM((bases * atoms, atoms + 2 * ghosts), f32),
        pltpu.VMEM((bases * atoms, atoms + 2 * ghosts), bf16),
        pltpu.VMEM((3 * part_rows, domains * atoms), bf16),
        pltpu.VMEM((part_rows, wave_count // 2), f32),
        pltpu.VMEM((wave_count, domains * atoms), bf16),
        pltpu.VMEM((2 * atoms, wave_count), bf16),
        pltpu.VMEM((wave_count, width), bf16),
        pltpu.VMEM((2, 2, atoms, width), f32),
        pltpu.VMEM((2, atoms, width), f32),
        pltpu.VMEM((count_a, width), f32),
        pltpu.VMEM((count_b, width), f32),
        pltpu.VMEM((devices, part_rows, width), f32),
        pltpu.VMEM((devices, part_rows, width), f32),
        pltpu.VMEM((count_a, width), f32),
        pltpu.VMEM((count_b, width), f32),
        pltpu.VMEM((part_rows, width), f32),
        pltpu.VMEM((part_rows, width), f32),
        pltpu.SemaphoreType.DMA((3, chips)),
        pltpu.SemaphoreType.DMA((3, chips)),
        pltpu.SemaphoreType.DMA((3, chips)),
        pltpu.SemaphoreType.DMA((3, chips)),
        pltpu.SemaphoreType.DMA((4,)),
        pltpu.SemaphoreType.DMA((4,)),
        pltpu.SemaphoreType.DMA((2,)),
        pltpu.SemaphoreType.DMA((2,)),
        pltpu.SemaphoreType.DMA((4,)),
        pltpu.SemaphoreType.DMA((4,)),
    ]
    shape = jax.ShapeDtypeStruct
    return pl.pallas_call(
        functools.partial(block_kernel, domains, cells),
        out_shape=(
            shape(feats.shape, bf16),
            shape(feats.shape, bf16),
            shape((width, width), f32),
            shape((width, width), f32),
            shape((bases, width), f32),
            shape((width, width), f32),
        ),
        in_specs=[vmem] * 17,
        out_specs=(vmem,) * 6,
        scratch_shapes=scratch,
        compiler_params=pltpu.CompilerParams(
            collective_id=0, has_side_effects=True, vmem_limit_bytes=48 * 1024 * 1024
        ),
        name="ewald_block",
    )(
        feats,
        positions,
        species,
        wave_vectors,
        smearing[None, :],
        species_gain,
        w_charge,
        w_message,
        w_radial,
        w_out,
        edge_sender,
        edge_receiver,
        edge_mask,
        edge_length,
        ghost_down,
        ghost_up,
        cotangent,
    )


def solution(mesh):
    placed = (
        P("cell", "dom", None),
        P("cell", None, "dom"),
        P("cell", "dom"),
        P(),
        P(),
        P(),
        P(),
        P(),
        P(),
        P(),
        P("cell", "dom"),
        P("cell", "dom"),
        P("cell", "dom"),
        P("cell", "dom"),
        P("cell", "dom"),
        P("cell", "dom"),
        P("cell", "dom", None),
    )
    return jax.shard_map(
        per_device,
        mesh=mesh,
        in_specs=placed,
        out_specs=(P("cell", "dom", None), P("cell", "dom", None), P(), P(), P(), P()),
        check_vma=False,
    )
```

```python
import math

import jax
import jax.numpy as jnp
from jax import lax
from jax.experimental import pallas as pl
from jax.experimental.pallas import tpu as pltpu
from jax.sharding import PartitionSpec as P

cutoff_radius = 6.0
basis_width = 0.75
edge_scale = 0.25
filter_factor = 12.0
MESH = pl.DeviceIdType.MESH
edge_chunk = 1024
wave_chunk = 128
lane = 128
part_rows = 8

sine_terms = (32.78140079, -74.47800454, 81.36681529, -41.33121431, 6.2830558)
cosine_terms = (-21.07678176, 58.79403849, -85.27239696, 64.92872661, -19.73898252, 0.99999922)


def horner(terms, x):
    value = terms[0] * x + terms[1]
    for term in terms[2:]:
        value = value * x + term
    return value


def dot(left, right, dims, precision=None):
    return lax.dot_general(
        left, right, (dims, ((), ())), preferred_element_type=jnp.float32, precision=precision
    )


def rows_by_rows(left, right):
    return dot(left, right, ((0,), (0,)))


def plain(left, right):
    return dot(left, right, ((1,), (0,)))


def by_transpose(left, right):
    return dot(left, right, ((1,), (1,)))


def edge_weights(length, mask, bases):
    shape = (bases, length.shape[1])
    centers = 0.5 + basis_width * lax.broadcasted_iota(jnp.int32, shape, 0).astype(jnp.float32)
    basis = jnp.exp(-jnp.square((length - centers) / basis_width))
    turn = math.pi * (length / cutoff_radius - 0.5)
    square = turn * turn
    sine = turn * horner(
        (-1.0 / 39916800.0, 1.0 / 362880.0, -1.0 / 5040.0, 1.0 / 120.0, -1.0 / 6.0, 1.0), square
    )
    return (basis * (0.5 * (1.0 - sine) * mask.astype(jnp.float32))).astype(jnp.bfloat16)


def spread(index, rows):
    shape = (rows, index.shape[1])
    return lax.broadcasted_iota(jnp.int32, shape, 0) == index


def block_kernel(
    domains,
    cells,
    sources,
    staged,
    updated_ref,
    feat_grad_ref,
    grad_charge_ref,
    grad_message_ref,
    grad_radial_ref,
    grad_out_ref,
    pos_all,
    charge_all,
    grad_all,
    outgoing,
    extended,
    returning,
    returned,
    pair_total,
    pairs,
    filt,
    structure,
    wave_rows,
    wave_columns,
    table,
    own_table,
    field,
    half_out,
    half_in,
    sums_a,
    sums_b,
    slots_a,
    slots_b,
    reduced_a,
    reduced_b,
    owned_a,
    owned_b,
    gather_send,
    gather_recv,
    pass_send,
    pass_recv,
    side_send,
    side_recv,
    half_send,
    half_recv,
    weight_send,
    weight_recv,
    load,
):
    (
        feats,
        positions,
        species,
        waves,
        smearing,
        species_gain,
        w_charge,
        w_message,
        w_radial,
        w_out,
        senders,
        receivers,
        mask,
        lengths,
        ghost_down,
        ghost_up,
        cotangent,
    ) = staged
    atoms = feats.shape[1]
    ghosts = ghost_down.shape[1]
    bases = w_radial.shape[0]
    wave_count = waves.shape[1]
    half = wave_count // 2
    chips = domains // 2
    devices = domains * cells
    inv_waves = 1.0 / math.sqrt(wave_count)
    inv_atoms = 1.0 / math.sqrt(atoms * domains)
    grad_scale = 1.0 / math.sqrt(cells * atoms * domains)

    cell = lax.axis_index("cell")
    me = lax.axis_index("dom")
    core = lax.rem(me, 2)
    chip = lax.div(me, 2)
    partner = me + 1 - 2 * core
    linear = cell * domains + me

    def place(index):
        return (lax.div(index, domains), lax.rem(index, domains))

    loads = [
        pltpu.make_async_copy(source, target, load.at[index])
        for index, (source, target) in enumerate(zip(sources, staged))
    ]
    for copy in loads:
        copy.start()

    barrier = pltpu.get_barrier_semaphore()

    def greet(step, carry):
        target = lax.rem(linear + step, devices)
        pl.semaphore_signal(barrier, inc=1, device_id=place(target), device_id_type=MESH)
        return carry

    lax.fori_loop(1, devices, greet, 0, unroll=devices <= 32)

    def remote(source, target, send, recv, index):
        return pltpu.make_async_remote_copy(
            src_ref=source,
            dst_ref=target,
            send_sem=send,
            recv_sem=recv,
            device_id=(cell, index),
            device_id_type=MESH,
        )

    for copy in loads:
        copy.wait()
    rows = feats[0]
    upstream_cot = cotangent[0]
    pos_all[me] = jnp.zeros(pos_all.shape[1:], jnp.float32)
    pos_all[me, 0:3, :] = positions[:, 0, :]
    kinds = spread(species[...], species_gain.shape[0]).astype(jnp.float32)
    gain = dot(kinds, species_gain[...], ((0,), (0,)), lax.Precision.HIGHEST)
    charge_all[me] = (plain(rows, w_charge[...]) * gain).astype(jnp.bfloat16)
    down_spread = spread(ghost_down[...], atoms).astype(jnp.bfloat16)
    up_spread = spread(ghost_up[...], atoms).astype(jnp.bfloat16)
    outgoing[0] = rows_by_rows(up_spread, rows).astype(jnp.bfloat16)
    outgoing[1] = rows_by_rows(down_spread, rows).astype(jnp.bfloat16)
    extended[0:atoms, :] = rows

    pl.semaphore_wait(barrier, devices - 1)

    def gather_copy(buffer, which, step, index):
        return remote(
            buffer.at[index],
            buffer.at[index],
            gather_send.at[which, step],
            gather_recv.at[which, step],
            lax.rem(chip + step, chips) * 2 + core,
        )

    def pass_copy(buffer, which, step, index):
        return remote(
            buffer.at[index],
            buffer.at[index],
            pass_send.at[which, step],
            pass_recv.at[which, step],
            partner,
        )

    def gather_start(buffer, which):
        pass_copy(buffer, which, 0, me).start()
        for step in range(1, chips):
            gather_copy(buffer, which, step, me).start()

    def chip_at(step):
        return lax.rem(chip - step + chips, chips)

    def gather_pass(buffer, which, step):
        source = chip_at(step) * 2 + core
        gather_copy(buffer, which, step, source).wait_recv()
        pass_copy(buffer, which, step, source).start()

    def gather_wait(buffer, which, step):
        pass_copy(buffer, which, step, chip_at(step) * 2 + (1 - core)).wait_recv()

    def gather_end(buffer, which):
        for step in range(1, chips):
            gather_copy(buffer, which, step, me).wait_send()
        for step in range(chips):
            pass_copy(buffer, which, step, me).wait_send()

    gather_start(pos_all, 0)
    gather_start(charge_all, 1)
    above = lax.rem(me + 1, domains)
    below = lax.rem(me + domains - 1, domains)
    low = pl.ds(atoms, ghosts)
    high = pl.ds(atoms + ghosts, ghosts)
    ghost_copies = [
        remote(outgoing.at[0], extended.at[low], side_send.at[0], side_recv.at[0], above),
        remote(outgoing.at[1], extended.at[high], side_send.at[1], side_recv.at[1], below),
    ]
    for copy in ghost_copies:
        copy.start()

    pair_total[...] = jnp.zeros_like(pair_total)

    def edge_step(step, carry):
        at = pl.ds(pl.multiple_of(step * edge_chunk, edge_chunk), edge_chunk)
        weights = edge_weights(lengths[:, at], mask[:, at], bases)
        receiver = spread(receivers[:, at], atoms).astype(jnp.bfloat16)
        sender = spread(senders[:, at], atoms + 2 * ghosts).astype(jnp.bfloat16)
        left = jnp.concatenate([receiver * weights[b : b + 1] for b in range(bases)], axis=0)
        pair_total[...] += by_transpose(left, sender)
        return carry

    edge_steps = lengths.shape[1] // edge_chunk
    early_steps = edge_steps * 2 // 3
    lax.fori_loop(0, early_steps, edge_step, 0)
    for step in range(1, chips):
        gather_pass(pos_all, 0, step)
    for step in range(1, chips):
        gather_pass(charge_all, 1, step)
    lax.fori_loop(early_steps, edge_steps, edge_step, 0)
    pairs[...] = pair_total[...].astype(jnp.bfloat16)

    wave_rows[...] = jnp.zeros_like(wave_rows)
    wave_rows[0:3, :] = waves[:, pl.ds(pl.multiple_of(core * half, lane), half)].astype(jnp.float32)
    ones = jnp.ones((part_rows, lane), jnp.bfloat16)
    wave = wave_rows[...]
    squared = rows_by_rows((wave * wave).astype(jnp.bfloat16), ones)
    filt[...] = filter_factor * jnp.exp(-squared * smearing[...]) * lax.rsqrt(squared)
    wave_columns[...] = jnp.concatenate([wave, wave, wave], axis=0).T.astype(jnp.bfloat16)
    pair = 2 * atoms

    def pair_of(step):
        return pl.ds(chip_at(step) * 2, 2)

    def columns(step):
        return pl.ds(pl.multiple_of(step * pair, lane), pair)

    def table_step(step, carry):
        gather_wait(pos_all, 0, step)
        block = pos_all[pair_of(step)]
        exact = jnp.concatenate([block[0], block[1]], axis=1)
        first = exact.astype(jnp.bfloat16).astype(jnp.float32)
        rest = exact - first
        second = rest.astype(jnp.bfloat16).astype(jnp.float32)
        points = jnp.concatenate([first, second, rest - second], axis=0).astype(jnp.bfloat16)
        at = columns(step)
        for low_row in range(0, half, wave_chunk):
            piece = slice(low_row, low_row + wave_chunk)
            turns = plain(wave_columns[piece, :], points)
            turns = turns - jnp.floor(turns + 0.5)
            square = turns * turns
            table[piece, at] = horner(cosine_terms, square).astype(jnp.bfloat16)
            table[half + low_row : half + low_row + wave_chunk, at] = (
                turns * horner(sine_terms, square)
            ).astype(jnp.bfloat16)
        gather_wait(charge_all, 1, step)
        structure[...] += plain(table[:, at], charge_all[pair_of(step)].reshape(pair, -1))
        return carry

    structure[...] = jnp.zeros_like(structure)
    lax.fori_loop(0, chips, table_step, 0)
    own_table[...] = table[:, 0:pair].T

    def fill_field(scale):
        scaled = filt[...] * scale
        field[0:half, :] = (scaled * structure[0:half, :]).astype(jnp.bfloat16)
        field[half:, :] = (scaled * structure[half:, :]).astype(jnp.bfloat16)

    fill_field(inv_atoms)
    gather_end(pos_all, 0)
    gather_end(charge_all, 1)

    def exchange(which):
        partial = plain(own_table[...], field[...])
        half_out[which] = partial.reshape(2, atoms, -1)
        copy = remote(
            half_out.at[which, 1 - core],
            half_in.at[which],
            half_send.at[which],
            half_recv.at[which],
            partner,
        )
        copy.start()
        return copy

    first_exchange = exchange(0)
    for copy in ghost_copies:
        copy.wait()
    message_rows = plain(extended[...], w_message[...]).astype(jnp.bfloat16)
    mixed = plain(pairs[...], message_rows).reshape(bases, atoms, -1)
    aggregate = jnp.zeros((atoms, rows.shape[1]), jnp.float32)
    for b in range(bases):
        aggregate += w_radial[b : b + 1, :] * mixed[b]
    grad_act = by_transpose(upstream_cot, w_out[...])
    first_exchange.wait()
    potential = (half_out[0, core] + half_in[0]) * inv_waves
    preact = aggregate * edge_scale + potential
    sig = 1.0 / (1.0 + jnp.exp(-preact))
    grad_pre = grad_act * sig * (1.0 + preact * (1.0 - sig))
    grad_all[me] = grad_pre.astype(jnp.bfloat16)
    gather_start(grad_all, 2)

    act = (preact * sig).astype(jnp.bfloat16)
    updated_ref[0] = (rows.astype(jnp.float32) + plain(act, w_out[...])).astype(jnp.bfloat16)
    scaled_pre = edge_scale * grad_pre
    weighted = jnp.concatenate(
        [(w_radial[b : b + 1, :] * scaled_pre).astype(jnp.bfloat16) for b in range(bases)], axis=0
    )
    grad_msg = rows_by_rows(pairs[...], weighted).astype(jnp.bfloat16)
    grad_rows = by_transpose(grad_msg, w_message[...])
    returning[...] = grad_rows[atoms:].reshape(returning.shape)
    return_copies = [
        remote(returning.at[0], returned.at[0], side_send.at[2], side_recv.at[2], below),
        remote(returning.at[1], returned.at[1], side_send.at[3], side_recv.at[3], above),
    ]
    for copy in return_copies:
        copy.start()
    sums_a[0:atoms_of(sums_a), :] = rows_by_rows(extended[...], grad_msg)
    sums_a[atoms_of(sums_a) :, :] = rows_by_rows(act, upstream_cot)

    def scatter_start(sums, slots, which):
        owners = sums.shape[0] // part_rows
        slots[linear] = jnp.zeros(slots.shape[1:], jnp.float32)

        def send(step, carry):
            target = lax.rem(linear + step, devices)

            @pl.when(target < owners)
            def _():
                pltpu.make_async_remote_copy(
                    src_ref=sums.at[pl.ds(pl.multiple_of(target * part_rows, part_rows), part_rows)],
                    dst_ref=slots.at[linear],
                    send_sem=weight_send.at[which],
                    recv_sem=weight_recv.at[which],
                    device_id=place(target),
                    device_id_type=MESH,
                ).start()

            return carry

        lax.fori_loop(1, devices, send, 0, unroll=devices <= 32)

    def wait_bytes(ref, send, recv):
        return pltpu.make_async_remote_copy(
            src_ref=ref,
            dst_ref=ref,
            send_sem=send,
            recv_sem=recv,
            device_id=(cell, partner),
            device_id_type=MESH,
        )

    def scatter_finish(sums, slots, owned, reduced, which):
        owners = sums.shape[0] // part_rows
        mine = pl.ds(pl.multiple_of(lax.rem(linear, owners) * part_rows, part_rows), part_rows)
        send, recv = weight_send.at[which], weight_recv.at[which]

        @pl.when(linear < owners)
        def _():
            wait_bytes(slots.at[pl.ds(0, devices - 1)], send, recv).wait_recv()
            wait_bytes(sums.at[pl.ds(0, (owners - 1) * part_rows)], send, recv).wait_send()
            total = sums[mine, :]
            for index in range(devices):
                total += slots[index]
            owned[...] = total * grad_scale
            reduced[mine, :] = owned[...]

        @pl.when(linear >= owners)
        def _():
            wait_bytes(sums, send, recv).wait_send()

    def share_start(owned, reduced, which):
        owners = reduced.shape[0] // part_rows

        @pl.when(linear < owners)
        def _():
            def send(step, carry):
                target = lax.rem(linear + step, devices)
                pltpu.make_async_remote_copy(
                    src_ref=owned,
                    dst_ref=reduced.at[
                        pl.ds(
                            pl.multiple_of(lax.rem(linear, owners) * part_rows, part_rows),
                            part_rows,
                        )
                    ],
                    send_sem=weight_send.at[which + 1],
                    recv_sem=weight_recv.at[which + 1],
                    device_id=place(target),
                    device_id_type=MESH,
                ).start()
                return carry

            lax.fori_loop(1, devices, send, 0, unroll=devices <= 32)

    def share_finish(slots, reduced, which):
        owners = reduced.shape[0] // part_rows
        send, recv = weight_send.at[which + 1], weight_recv.at[which + 1]

        @pl.when(linear < owners)
        def _():
            wait_bytes(reduced.at[pl.ds(0, (owners - 1) * part_rows)], send, recv).wait_recv()
            wait_bytes(slots.at[pl.ds(0, devices - 1)], send, recv).wait_send()

        @pl.when(linear >= owners)
        def _():
            wait_bytes(reduced, send, recv).wait_recv()

    scatter_start(sums_a, slots_a, 0)

    grad_radial = jnp.concatenate(
        [jnp.sum(mixed[b] * scaled_pre, axis=0, keepdims=True) for b in range(bases)], axis=0
    )
    sums_b[pl.ds(sums_b.shape[0] - bases, bases), :] = grad_radial

    ahead = min(2, chips - 1)
    for step in range(1, ahead + 1):
        gather_pass(grad_all, 2, step)
    structure[...] = jnp.zeros_like(structure)

    def back_step(step, carry):
        @pl.when(step + ahead < chips)
        def _():
            @pl.when(step > 0)
            def _():
                gather_pass(grad_all, 2, step + ahead)

        gather_wait(grad_all, 2, step)
        structure[...] += plain(
            table[:, columns(step)], grad_all[pair_of(step)].reshape(pair, -1)
        )
        return carry

    lax.fori_loop(0, chips, back_step, 0)
    fill_field(inv_waves * inv_atoms)
    gather_end(grad_all, 2)
    second_exchange = exchange(1)

    scatter_finish(sums_a, slots_a, owned_a, reduced_a, 0)
    share_start(owned_a, reduced_a, 0)

    second_exchange.wait()
    grad_raw = ((half_out[1, core] + half_in[1]) * gain).astype(jnp.bfloat16)
    sums_b[0 : sums_b.shape[0] - bases, :] = rows_by_rows(rows, grad_raw)
    scatter_start(sums_b, slots_b, 2)
    for copy in return_copies:
        copy.wait()
    total = (
        upstream_cot.astype(jnp.float32)
        + by_transpose(grad_raw, w_charge[...])
        + grad_rows[:atoms]
        + dot(down_spread.astype(jnp.float32), returned[1], ((1,), (0,)), lax.Precision.HIGHEST)
        + dot(up_spread.astype(jnp.float32), returned[0], ((1,), (0,)), lax.Precision.HIGHEST)
    )
    feat_grad_ref[0] = total.astype(jnp.bfloat16)

    scatter_finish(sums_b, slots_b, owned_b, reduced_b, 2)
    share_start(owned_b, reduced_b, 2)
    share_finish(slots_a, reduced_a, 0)
    grad_message_ref[...] = reduced_a[0 : atoms_of(sums_a), :]
    grad_out_ref[...] = reduced_a[atoms_of(sums_a) :, :]
    share_finish(slots_b, reduced_b, 2)
    grad_charge_ref[...] = reduced_b[0 : sums_b.shape[0] - bases, :]
    grad_radial_ref[...] = reduced_b[sums_b.shape[0] - bases :, :]


def atoms_of(sums):
    return sums.shape[0] // 2


def write_kernel(*refs):
    done = refs[-1]
    count = len(refs) // 2
    copies = [
        pltpu.make_async_copy(refs[index], refs[count + index], done.at[index])
        for index in range(count)
    ]
    for copy in copies:
        copy.start()
    for copy in copies:
        copy.wait()


def per_device(
    feats,
    positions,
    species,
    wave_vectors,
    smearing,
    species_gain,
    w_charge,
    w_message,
    w_radial,
    w_out,
    edge_sender,
    edge_receiver,
    edge_mask,
    edge_length,
    ghost_down,
    ghost_up,
    cotangent,
):
    domains = lax.axis_size("dom")
    cells = lax.axis_size("cell")
    atoms, width = feats.shape[1:]
    ghosts = ghost_down.shape[1]
    bases = w_radial.shape[0]
    wave_count = wave_vectors.shape[1]
    devices = domains * cells
    chips = domains // 2
    f32, bf16 = jnp.float32, jnp.bfloat16
    vmem = pl.BlockSpec(memory_space=pltpu.VMEM)
    count_a = 2 * width
    count_b = width + bases
    scratch = [
        pltpu.VMEM((domains, part_rows, atoms), f32),
        pltpu.VMEM((domains, atoms, width), bf16),
        pltpu.VMEM((domains, atoms, width), bf16),
        pltpu.VMEM((2, ghosts, width), bf16),
        pltpu.VMEM((atoms + 2 * ghosts, width), bf16),
        pltpu.VMEM((2, ghosts, width), f32),
        pltpu.VMEM((2, ghosts, width), f32),
        pltpu.VMEM((bases * atoms, atoms + 2 * ghosts), f32),
        pltpu.VMEM((bases * atoms, atoms + 2 * ghosts), bf16),
        pltpu.VMEM((wave_count // 2, width), f32),
        pltpu.VMEM((wave_count, width), f32),
        pltpu.VMEM((part_rows, wave_count // 2), f32),
        pltpu.VMEM((wave_count // 2, 3 * part_rows), bf16),
        pltpu.VMEM((wave_count, domains * atoms), bf16),
        pltpu.VMEM((2 * atoms, wave_count), bf16),
        pltpu.VMEM((wave_count, width), bf16),
        pltpu.VMEM((2, 2, atoms, width), f32),
        pltpu.VMEM((2, atoms, width), f32),
        pltpu.VMEM((count_a, width), f32),
        pltpu.VMEM((count_b, width), f32),
        pltpu.VMEM((devices, part_rows, width), f32),
        pltpu.VMEM((devices, part_rows, width), f32),
        pltpu.VMEM((count_a, width), f32),
        pltpu.VMEM((count_b, width), f32),
        pltpu.VMEM((part_rows, width), f32),
        pltpu.VMEM((part_rows, width), f32),
        pltpu.SemaphoreType.DMA((3, chips)),
        pltpu.SemaphoreType.DMA((3, chips)),
        pltpu.SemaphoreType.DMA((3, chips)),
        pltpu.SemaphoreType.DMA((3, chips)),
        pltpu.SemaphoreType.DMA((4,)),
        pltpu.SemaphoreType.DMA((4,)),
        pltpu.SemaphoreType.DMA((2,)),
        pltpu.SemaphoreType.DMA((2,)),
        pltpu.SemaphoreType.DMA((4,)),
        pltpu.SemaphoreType.DMA((4,)),
    ]
    shape = jax.ShapeDtypeStruct
    operands = (
        feats,
        positions.transpose(1, 0, 2),
        species,
        wave_vectors,
        smearing[None, :],
        species_gain,
        w_charge,
        w_message,
        w_radial,
        w_out,
        edge_sender,
        edge_receiver,
        edge_mask,
        edge_length,
        ghost_down,
        ghost_up,
        cotangent,
    )
    count = len(operands)
    staged = [pltpu.VMEM(value.shape, value.dtype) for value in operands]
    scratch = [*staged, *scratch, pltpu.SemaphoreType.DMA((count,))]
    outs = (
        shape(feats.shape, bf16),
        shape(feats.shape, bf16),
        shape((width, width), f32),
        shape((width, width), f32),
        shape((bases, width), f32),
        shape((width, width), f32),
    )

    def body(*refs):
        sources, rest = refs[:count], refs[count:]
        results, rest = rest[: len(outs)], rest[len(outs) :]
        block_kernel(domains, cells, sources, rest[:count], *results, *rest[count:])

    results = pl.pallas_call(
        body,
        out_shape=outs,
        in_specs=[pl.BlockSpec(memory_space=pltpu.HBM)] * count,
        out_specs=(vmem,) * len(outs),
        scratch_shapes=scratch,
        compiler_params=pltpu.CompilerParams(
            collective_id=0, has_side_effects=True, vmem_limit_bytes=64 * 1024 * 1024
        ),
        name="ewald_block",
    )(*operands)
    return pl.pallas_call(
        write_kernel,
        out_shape=outs,
        in_specs=[pl.BlockSpec(memory_space=pltpu.HBM)] * len(outs),
        out_specs=(pl.BlockSpec(memory_space=pltpu.HBM),) * len(outs),
        scratch_shapes=[pltpu.SemaphoreType.DMA((len(outs),))],
        compiler_params=pltpu.CompilerParams(vmem_limit_bytes=64 * 1024 * 1024),
        name="write_out",
    )(*results)


def solution(mesh):
    placed = (
        P("cell", "dom", None),
        P("cell", None, "dom"),
        P("cell", "dom"),
        P(),
        P(),
        P(),
        P(),
        P(),
        P(),
        P(),
        P("cell", "dom"),
        P("cell", "dom"),
        P("cell", "dom"),
        P("cell", "dom"),
        P("cell", "dom"),
        P("cell", "dom"),
        P("cell", "dom", None),
    )
    return jax.shard_map(
        per_device,
        mesh=mesh,
        in_specs=placed,
        out_specs=(P("cell", "dom", None), P("cell", "dom", None), P(), P(), P(), P()),
        check_vma=False,
    )
```

```python
import math

import jax
import jax.numpy as jnp
from jax import lax
from jax.experimental import pallas as pl
from jax.experimental.pallas import tpu as pltpu
from jax.sharding import PartitionSpec as P

cutoff_radius = 6.0
basis_width = 0.75
edge_scale = 0.25
filter_factor = 12.0
MESH = pl.DeviceIdType.MESH
edge_chunk = 2048
wave_chunk = 128
lane = 128
part_rows = 16
coord_rows = 8

sine_terms = (32.78140079, -74.47800454, 81.36681529, -41.33121431, 6.2830558)
cosine_terms = (-21.07678176, 58.79403849, -85.27239696, 64.92872661, -19.73898252, 0.99999922)


def horner(terms, x):
    value = terms[0] * x + terms[1]
    for term in terms[2:]:
        value = value * x + term
    return value


def dot(left, right, dims, precision=None):
    return lax.dot_general(
        left, right, (dims, ((), ())), preferred_element_type=jnp.float32, precision=precision
    )


def rows_by_rows(left, right):
    return dot(left, right, ((0,), (0,)))


def plain(left, right):
    return dot(left, right, ((1,), (0,)))


def by_transpose(left, right):
    return dot(left, right, ((1,), (1,)))


def edge_weights(length, mask, bases):
    shape = (bases, length.shape[1])
    centers = 0.5 + basis_width * lax.broadcasted_iota(jnp.int32, shape, 0).astype(jnp.float32)
    basis = jnp.exp(-jnp.square((length - centers) / basis_width))
    turn = math.pi * (length / cutoff_radius - 0.5)
    square = turn * turn
    sine = turn * horner(
        (-1.0 / 39916800.0, 1.0 / 362880.0, -1.0 / 5040.0, 1.0 / 120.0, -1.0 / 6.0, 1.0), square
    )
    return (basis * (0.5 * (1.0 - sine) * mask.astype(jnp.float32))).astype(jnp.bfloat16)


def spread(index, rows):
    shape = (rows, index.shape[1])
    return lax.broadcasted_iota(jnp.int32, shape, 0) == index


def block_kernel(
    domains,
    cells,
    sources,
    staged,
    updated_ref,
    feat_grad_ref,
    grad_charge_ref,
    grad_message_ref,
    grad_radial_ref,
    grad_out_ref,
    pos_all,
    charge_all,
    grad_all,
    outgoing,
    extended,
    returning,
    returned,
    pair_total,
    pairs,
    filt,
    structure,
    wave_rows,
    wave_columns,
    table,
    own_table,
    field,
    half_out,
    half_in,
    sums,
    slots,
    reduced,
    owned,
    gather_send,
    gather_recv,
    pass_send,
    pass_recv,
    side_send,
    side_recv,
    half_send,
    half_recv,
    weight_send,
    weight_recv,
    load,
):
    (
        feats,
        positions,
        species,
        waves,
        smearing,
        species_gain,
        w_charge,
        w_message,
        w_radial,
        w_out,
        senders,
        receivers,
        mask,
        lengths,
        ghost_down,
        ghost_up,
        cotangent,
    ) = staged
    atoms = feats.shape[1]
    ghosts = ghost_down.shape[1]
    bases = w_radial.shape[0]
    wave_count = waves.shape[1]
    half = wave_count // 2
    chips = domains // 2
    devices = domains * cells
    inv_waves = 1.0 / math.sqrt(wave_count)
    inv_atoms = 1.0 / math.sqrt(atoms * domains)
    grad_scale = 1.0 / math.sqrt(cells * atoms * domains)

    cell = lax.axis_index("cell")
    me = lax.axis_index("dom")
    core = lax.rem(me, 2)
    chip = lax.div(me, 2)
    partner = me + 1 - 2 * core
    linear = cell * domains + me

    def place(index):
        return (lax.div(index, domains), lax.rem(index, domains))

    loads = [
        pltpu.make_async_copy(source, target, load.at[index])
        for index, (source, target) in enumerate(zip(sources, staged))
    ]
    for copy in loads:
        copy.start()

    barrier = pltpu.get_barrier_semaphore()

    def greet(step, carry):
        target = lax.rem(linear + step, devices)
        pl.semaphore_signal(barrier, inc=1, device_id=place(target), device_id_type=MESH)
        return carry

    lax.fori_loop(1, devices, greet, 0, unroll=devices <= 32)

    def remote(source, target, send, recv, index):
        return pltpu.make_async_remote_copy(
            src_ref=source,
            dst_ref=target,
            send_sem=send,
            recv_sem=recv,
            device_id=(cell, index),
            device_id_type=MESH,
        )

    for index in (10, 11, 12, 13):
        loads[index].wait()

    pair_total[...] = jnp.zeros_like(pair_total)

    def edge_step(step, carry):
        at = pl.ds(pl.multiple_of(step * edge_chunk, edge_chunk), edge_chunk)
        weights = edge_weights(lengths[:, at], mask[:, at], bases)
        receiver = spread(receivers[:, at], atoms).astype(jnp.bfloat16)
        sender = spread(senders[:, at], atoms + 2 * ghosts).astype(jnp.bfloat16)
        left = jnp.concatenate([receiver * weights[b : b + 1] for b in range(bases)], axis=0)
        pair_total[...] += by_transpose(left, sender)
        return carry

    edge_step(0, 0)

    for index in (0, 1, 2, 3, 4, 5, 6, 7, 8, 9, 14, 15, 16):
        loads[index].wait()
    rows = feats[0]
    upstream_cot = cotangent[0]
    pos_all[me] = jnp.zeros(pos_all.shape[1:], jnp.float32)
    pos_all[me, 0:3, :] = positions[:, 0, :]
    kinds = spread(species[...], species_gain.shape[0]).astype(jnp.float32)
    gain = dot(kinds, species_gain[...], ((0,), (0,)), lax.Precision.HIGHEST)
    charge_all[me] = (plain(rows, w_charge[...]) * gain).astype(jnp.bfloat16)
    down_spread = spread(ghost_down[...], atoms).astype(jnp.bfloat16)
    up_spread = spread(ghost_up[...], atoms).astype(jnp.bfloat16)
    outgoing[0] = rows_by_rows(up_spread, rows).astype(jnp.bfloat16)
    outgoing[1] = rows_by_rows(down_spread, rows).astype(jnp.bfloat16)
    extended[0:atoms, :] = rows

    pl.semaphore_wait(barrier, devices - 1)

    def gather_copy(buffer, which, step, index):
        return remote(
            buffer.at[index],
            buffer.at[index],
            gather_send.at[which, step],
            gather_recv.at[which, step],
            lax.rem(chip + step, chips) * 2 + core,
        )

    def pass_copy(buffer, which, step, index):
        return remote(
            buffer.at[index],
            buffer.at[index],
            pass_send.at[which, step],
            pass_recv.at[which, step],
            partner,
        )

    def gather_start(buffer, which):
        pass_copy(buffer, which, 0, me).start()
        for step in range(1, chips):
            gather_copy(buffer, which, step, me).start()

    def chip_at(step):
        return lax.rem(chip - step + chips, chips)

    def gather_pass(buffer, which, step):
        source = chip_at(step) * 2 + core
        gather_copy(buffer, which, step, source).wait_recv()
        pass_copy(buffer, which, step, source).start()

    def gather_wait(buffer, which, step):
        pass_copy(buffer, which, step, chip_at(step) * 2 + (1 - core)).wait_recv()

    def gather_end(buffer, which):
        for step in range(1, chips):
            gather_copy(buffer, which, step, me).wait_send()
        for step in range(chips):
            pass_copy(buffer, which, step, me).wait_send()

    gather_start(pos_all, 0)
    gather_start(charge_all, 1)
    above = lax.rem(me + 1, domains)
    below = lax.rem(me + domains - 1, domains)
    low = pl.ds(atoms, ghosts)
    high = pl.ds(atoms + ghosts, ghosts)
    ghost_copies = [
        remote(outgoing.at[0], extended.at[low], side_send.at[0], side_recv.at[0], above),
        remote(outgoing.at[1], extended.at[high], side_send.at[1], side_recv.at[1], below),
    ]
    for copy in ghost_copies:
        copy.start()

    wave_rows[...] = jnp.zeros_like(wave_rows)
    wave_rows[0:3, :] = waves[:, pl.ds(pl.multiple_of(core * half, lane), half)].astype(jnp.float32)
    ones = jnp.ones((coord_rows, lane), jnp.bfloat16)
    wave = wave_rows[...]
    squared = rows_by_rows((wave * wave).astype(jnp.bfloat16), ones)
    filt[...] = filter_factor * jnp.exp(-squared * smearing[...]) * lax.rsqrt(squared)
    wave_columns[...] = jnp.concatenate([wave, wave, wave], axis=0).T.astype(jnp.bfloat16)
    pair = 2 * atoms

    def pair_of(step):
        return pl.ds(chip_at(step) * 2, 2)

    def columns(step):
        return pl.ds(pl.multiple_of(step * pair, lane), pair)

    def table_block(step):
        block = pos_all[pair_of(step)]
        exact = jnp.concatenate([block[0], block[1]], axis=1)
        first = exact.astype(jnp.bfloat16).astype(jnp.float32)
        rest = exact - first
        second = rest.astype(jnp.bfloat16).astype(jnp.float32)
        points = jnp.concatenate([first, second, rest - second], axis=0).astype(jnp.bfloat16)
        at = columns(step)
        for low_row in range(0, half, wave_chunk):
            piece = slice(low_row, low_row + wave_chunk)
            turns = plain(wave_columns[piece, :], points)
            turns = turns - jnp.floor(turns + 0.5)
            square = turns * turns
            table[piece, at] = horner(cosine_terms, square).astype(jnp.bfloat16)
            table[half + low_row : half + low_row + wave_chunk, at] = (
                turns * horner(sine_terms, square)
            ).astype(jnp.bfloat16)

    edge_steps = lengths.shape[1] // edge_chunk
    alone = 2
    shared = edge_steps - alone
    blocks = chips // shared
    assert blocks * shared == chips
    edge_step(1, 0)
    for step in range(1, chips):
        gather_pass(pos_all, 0, step)

    def shared_step(step, carry):
        for block in range(blocks):
            gather_wait(pos_all, 0, step * blocks + block)
        edge_step(alone + step, carry)
        for block in range(blocks):
            table_block(step * blocks + block)
        return carry

    lax.fori_loop(0, shared // 2, shared_step, 0)
    for step in range(1, chips):
        gather_pass(charge_all, 1, step)
    lax.fori_loop(shared // 2, shared, shared_step, 0)
    pairs[...] = pair_total[...].astype(jnp.bfloat16)

    def in_steps(buffer, steps):
        return jnp.concatenate([buffer[chip_at(step) * 2 + c] for step in steps for c in (0, 1)])

    for step in range(chips):
        gather_wait(charge_all, 1, step)
    structure[...] = plain(table[...], in_steps(charge_all, range(chips)))
    own_table[...] = table[:, 0:pair].T

    def fill_field(scale):
        scaled = filt[...] * scale
        field[0:half, :] = (scaled * structure[0:half, :]).astype(jnp.bfloat16)
        field[half:, :] = (scaled * structure[half:, :]).astype(jnp.bfloat16)

    fill_field(inv_atoms)
    gather_end(pos_all, 0)
    gather_end(charge_all, 1)

    def exchange(which):
        partial = plain(own_table[...], field[...])
        half_out[which] = partial.reshape(2, atoms, -1)
        copy = remote(
            half_out.at[which, 1 - core],
            half_in.at[which],
            half_send.at[which],
            half_recv.at[which],
            partner,
        )
        copy.start()
        return copy

    first_exchange = exchange(0)
    for copy in ghost_copies:
        copy.wait()
    message_rows = plain(extended[...], w_message[...]).astype(jnp.bfloat16)
    mixed = plain(pairs[...], message_rows).reshape(bases, atoms, -1)
    aggregate = jnp.zeros((atoms, rows.shape[1]), jnp.float32)
    for b in range(bases):
        aggregate += w_radial[b : b + 1, :] * mixed[b]
    grad_act = by_transpose(upstream_cot, w_out[...])
    first_exchange.wait()
    potential = (half_out[0, core] + half_in[0]) * inv_waves
    preact = aggregate * edge_scale + potential
    sig = 1.0 / (1.0 + jnp.exp(-preact))
    grad_pre = grad_act * sig * (1.0 + preact * (1.0 - sig))
    grad_all[me] = grad_pre.astype(jnp.bfloat16)
    gather_start(grad_all, 2)

    act = (preact * sig).astype(jnp.bfloat16)
    updated_ref[0] = (rows.astype(jnp.float32) + plain(act, w_out[...])).astype(jnp.bfloat16)
    scaled_pre = edge_scale * grad_pre
    weighted = jnp.concatenate(
        [(w_radial[b : b + 1, :] * scaled_pre).astype(jnp.bfloat16) for b in range(bases)], axis=0
    )
    grad_msg = rows_by_rows(pairs[...], weighted).astype(jnp.bfloat16)
    grad_rows = by_transpose(grad_msg, w_message[...])
    returning[...] = grad_rows[atoms:].reshape(returning.shape)
    return_copies = [
        remote(returning.at[0], returned.at[0], side_send.at[2], side_recv.at[2], below),
        remote(returning.at[1], returned.at[1], side_send.at[3], side_recv.at[3], above),
    ]
    for copy in return_copies:
        copy.start()
    width = rows.shape[1]
    sums[0:width, :] = rows_by_rows(extended[...], grad_msg).astype(jnp.bfloat16)
    sums[width : 2 * width, :] = rows_by_rows(act, upstream_cot).astype(jnp.bfloat16)
    grad_radial = [jnp.sum(mixed[b] * scaled_pre, axis=0, keepdims=True) for b in range(bases)]
    grad_radial.append(jnp.zeros((part_rows - bases, width), jnp.float32))
    sums[3 * width :, :] = jnp.concatenate(grad_radial, axis=0).astype(jnp.bfloat16)

    owners = sums.shape[0] // part_rows
    early = 2 * width // part_rows

    def part(ref, owner):
        return ref.at[pl.ds(pl.multiple_of(owner * part_rows, part_rows), part_rows)]

    def send_part(owner):
        return pltpu.make_async_remote_copy(
            src_ref=part(sums, owner),
            dst_ref=slots.at[linear],
            send_sem=weight_send.at[0],
            recv_sem=weight_recv.at[0],
            device_id=place(owner),
            device_id_type=MESH,
        )

    def scatter_start(first, last):
        for owner in range(first, last):

            @pl.when(linear != owner)
            def _():
                send_part(owner).start()

    def wait_bytes(ref, which):
        return pltpu.make_async_remote_copy(
            src_ref=ref,
            dst_ref=ref,
            send_sem=weight_send.at[which],
            recv_sem=weight_recv.at[which],
            device_id=(cell, partner),
            device_id_type=MESH,
        )

    def share():
        @pl.when(linear < owners)
        def _():
            wait_bytes(slots.at[pl.ds(0, devices - 1)], 0).wait_recv()
            slots[linear] = part(sums, linear)[...]
            total = slots[0].astype(jnp.float32)
            for index in range(1, devices):
                total += slots[index].astype(jnp.float32)
            owned[...] = (total * grad_scale).astype(jnp.bfloat16)

            def send(step, carry):
                pltpu.make_async_remote_copy(
                    src_ref=owned,
                    dst_ref=part(reduced, linear),
                    send_sem=weight_send.at[1],
                    recv_sem=weight_recv.at[1],
                    device_id=place(lax.rem(linear + step, devices)),
                    device_id_type=MESH,
                ).start()
                return carry

            lax.fori_loop(1, devices, send, 0, unroll=devices <= 32)
            part(reduced, linear)[...] = owned[...]

    def share_end():
        @pl.when(linear < owners)
        def _():
            wait_bytes(reduced.at[pl.ds(0, (owners - 1) * part_rows)], 1).wait_recv()
            wait_bytes(slots.at[pl.ds(0, devices - 1)], 1).wait_send()
            wait_bytes(sums.at[pl.ds(0, (owners - 1) * part_rows)], 0).wait_send()

        @pl.when(linear >= owners)
        def _():
            wait_bytes(reduced, 1).wait_recv()
            wait_bytes(sums, 0).wait_send()

    groups = 2
    size = chips // groups
    for step in range(1, size):
        gather_pass(grad_all, 2, step)
    for group in range(groups):
        steps = range(group * size, (group + 1) * size)
        if group + 1 < groups:
            for step in range((group + 1) * size, (group + 2) * size):
                gather_pass(grad_all, 2, step)
        for step in steps:
            gather_wait(grad_all, 2, step)
        update = plain(
            table[:, group * size * pair : (group + 1) * size * pair], in_steps(grad_all, steps)
        )
        structure[...] = update if group == 0 else structure[...] + update
    fill_field(inv_waves * inv_atoms)
    gather_end(grad_all, 2)
    second_exchange = exchange(1)

    scatter_start(0, early)
    second_exchange.wait()
    grad_raw = ((half_out[1, core] + half_in[1]) * gain).astype(jnp.bfloat16)
    sums[2 * width : 3 * width, :] = rows_by_rows(rows, grad_raw).astype(jnp.bfloat16)
    scatter_start(early, owners)
    for copy in return_copies:
        copy.wait()
    total = (
        upstream_cot.astype(jnp.float32)
        + by_transpose(grad_raw, w_charge[...])
        + grad_rows[:atoms]
        + dot(down_spread.astype(jnp.float32), returned[1], ((1,), (0,)), lax.Precision.HIGHEST)
        + dot(up_spread.astype(jnp.float32), returned[0], ((1,), (0,)), lax.Precision.HIGHEST)
    )
    feat_grad_ref[0] = total.astype(jnp.bfloat16)

    share()
    share_end()
    final = reduced[...].astype(jnp.float32)
    grad_message_ref[...] = final[0:width]
    grad_out_ref[...] = final[width : 2 * width]
    grad_charge_ref[...] = final[2 * width : 3 * width]
    grad_radial_ref[...] = final[3 * width : 3 * width + bases]


def write_kernel(*refs):
    count = len(refs) // 3
    sources, results, held, done = refs[:count], refs[count : 2 * count], refs[2 * count : -1], refs[-1]
    first = [
        pltpu.make_async_copy(sources[index], held[index], done.at[0, index])
        for index in range(count)
    ]
    second = [
        pltpu.make_async_copy(held[index], results[index], done.at[1, index])
        for index in range(count)
    ]
    for copy in first:
        copy.start()
    for copy, onward in zip(first, second):
        copy.wait()
        onward.start()
    for copy in second:
        copy.wait()


def per_device(
    feats,
    positions,
    species,
    wave_vectors,
    smearing,
    species_gain,
    w_charge,
    w_message,
    w_radial,
    w_out,
    edge_sender,
    edge_receiver,
    edge_mask,
    edge_length,
    ghost_down,
    ghost_up,
    cotangent,
):
    domains = lax.axis_size("dom")
    cells = lax.axis_size("cell")
    atoms, width = feats.shape[1:]
    ghosts = ghost_down.shape[1]
    bases = w_radial.shape[0]
    wave_count = wave_vectors.shape[1]
    devices = domains * cells
    chips = domains // 2
    f32, bf16 = jnp.float32, jnp.bfloat16
    vmem = pl.BlockSpec(memory_space=pltpu.VMEM)
    count = 3 * width + part_rows
    scratch = [
        pltpu.VMEM((domains, coord_rows, atoms), f32),
        pltpu.VMEM((domains, atoms, width), bf16),
        pltpu.VMEM((domains, atoms, width), bf16),
        pltpu.VMEM((2, ghosts, width), bf16),
        pltpu.VMEM((atoms + 2 * ghosts, width), bf16),
        pltpu.VMEM((2, ghosts, width), f32),
        pltpu.VMEM((2, ghosts, width), f32),
        pltpu.VMEM((bases * atoms, atoms + 2 * ghosts), f32),
        pltpu.VMEM((bases * atoms, atoms + 2 * ghosts), bf16),
        pltpu.VMEM((wave_count // 2, width), f32),
        pltpu.VMEM((wave_count, width), f32),
        pltpu.VMEM((coord_rows, wave_count // 2), f32),
        pltpu.VMEM((wave_count // 2, 3 * coord_rows), bf16),
        pltpu.VMEM((wave_count, domains * atoms), bf16),
        pltpu.VMEM((2 * atoms, wave_count), bf16),
        pltpu.VMEM((wave_count, width), bf16),
        pltpu.VMEM((2, 2, atoms, width), f32),
        pltpu.VMEM((2, atoms, width), f32),
        pltpu.VMEM((count, width), bf16),
        pltpu.VMEM((devices, part_rows, width), bf16),
        pltpu.VMEM((count, width), bf16),
        pltpu.VMEM((part_rows, width), bf16),
        pltpu.SemaphoreType.DMA((3, chips)),
        pltpu.SemaphoreType.DMA((3, chips)),
        pltpu.SemaphoreType.DMA((3, chips)),
        pltpu.SemaphoreType.DMA((3, chips)),
        pltpu.SemaphoreType.DMA((4,)),
        pltpu.SemaphoreType.DMA((4,)),
        pltpu.SemaphoreType.DMA((2,)),
        pltpu.SemaphoreType.DMA((2,)),
        pltpu.SemaphoreType.DMA((2,)),
        pltpu.SemaphoreType.DMA((2,)),
    ]
    shape = jax.ShapeDtypeStruct
    operands = (
        feats,
        positions.transpose(1, 0, 2),
        species,
        wave_vectors,
        smearing[None, :],
        species_gain,
        w_charge,
        w_message,
        w_radial,
        w_out,
        edge_sender,
        edge_receiver,
        edge_mask,
        edge_length,
        ghost_down,
        ghost_up,
        cotangent,
    )
    count = len(operands)
    staged = [pltpu.VMEM(value.shape, value.dtype) for value in operands]
    scratch = [*staged, *scratch, pltpu.SemaphoreType.DMA((count,))]
    outs = (
        shape(feats.shape, bf16),
        shape(feats.shape, bf16),
        shape((width, width), f32),
        shape((width, width), f32),
        shape((bases, width), f32),
        shape((width, width), f32),
    )

    def body(*refs):
        sources, rest = refs[:count], refs[count:]
        results, rest = rest[: len(outs)], rest[len(outs) :]
        block_kernel(domains, cells, sources, rest[:count], *results, *rest[count:])

    results = pl.pallas_call(
        body,
        out_shape=outs,
        in_specs=[pl.BlockSpec(memory_space=pltpu.HBM)] * count,
        out_specs=(vmem,) * len(outs),
        scratch_shapes=scratch,
        compiler_params=pltpu.CompilerParams(
            collective_id=0, has_side_effects=True, vmem_limit_bytes=64 * 1024 * 1024
        ),
        name="ewald_block",
    )(*operands)
    return pl.pallas_call(
        write_kernel,
        out_shape=outs,
        in_specs=[pl.BlockSpec(memory_space=pltpu.HBM)] * len(outs),
        out_specs=(pl.BlockSpec(memory_space=pltpu.HBM),) * len(outs),
        scratch_shapes=[
            *[pltpu.VMEM(out.shape, out.dtype) for out in outs],
            pltpu.SemaphoreType.DMA((2, len(outs))),
        ],
        compiler_params=pltpu.CompilerParams(vmem_limit_bytes=64 * 1024 * 1024),
        name="write_out",
    )(*results)


def solution(mesh):
    placed = (
        P("cell", "dom", None),
        P("cell", None, "dom"),
        P("cell", "dom"),
        P(),
        P(),
        P(),
        P(),
        P(),
        P(),
        P(),
        P("cell", "dom"),
        P("cell", "dom"),
        P("cell", "dom"),
        P("cell", "dom"),
        P("cell", "dom"),
        P("cell", "dom"),
        P("cell", "dom", None),
    )
    return jax.shard_map(
        per_device,
        mesh=mesh,
        in_specs=placed,
        out_specs=(P("cell", "dom", None), P("cell", "dom", None), P(), P(), P(), P()),
        check_vma=False,
    )
```

```python
import math

import jax
import jax.numpy as jnp
from jax import lax
from jax.experimental import pallas as pl
from jax.experimental.pallas import tpu as pltpu
from jax.sharding import PartitionSpec as P

cutoff_radius = 6.0
basis_width = 0.75
edge_scale = 0.25
filter_factor = 12.0
MESH = pl.DeviceIdType.MESH
edge_chunk = 1024
wave_chunk = 128
lane = 128
part_rows = 16
coord_rows = 8

sine_terms = (32.78140079, -74.47800454, 81.36681529, -41.33121431, 6.2830558)
cosine_terms = (-21.07678176, 58.79403849, -85.27239696, 64.92872661, -19.73898252, 0.99999922)


def horner(terms, x):
    value = terms[0] * x + terms[1]
    for term in terms[2:]:
        value = value * x + term
    return value


def dot(left, right, dims, precision=None):
    return lax.dot_general(
        left, right, (dims, ((), ())), preferred_element_type=jnp.float32, precision=precision
    )


def rows_by_rows(left, right):
    return dot(left, right, ((0,), (0,)))


def plain(left, right):
    return dot(left, right, ((1,), (0,)))


def by_transpose(left, right):
    return dot(left, right, ((1,), (1,)))


def edge_weights(length, mask, bases):
    shape = (bases, length.shape[1])
    centers = 0.5 + basis_width * lax.broadcasted_iota(jnp.int32, shape, 0).astype(jnp.float32)
    basis = jnp.exp(-jnp.square((length - centers) / basis_width))
    turn = math.pi * (length / cutoff_radius - 0.5)
    square = turn * turn
    sine = turn * horner(
        (-1.0 / 39916800.0, 1.0 / 362880.0, -1.0 / 5040.0, 1.0 / 120.0, -1.0 / 6.0, 1.0), square
    )
    return (basis * (0.5 * (1.0 - sine) * mask.astype(jnp.float32))).astype(jnp.bfloat16)


def spread(index, rows):
    shape = (rows, index.shape[1])
    return lax.broadcasted_iota(jnp.int32, shape, 0) == index


def block_kernel(
    domains,
    cells,
    sources,
    staged,
    updated_ref,
    feat_grad_ref,
    grad_charge_ref,
    grad_message_ref,
    grad_radial_ref,
    grad_out_ref,
    pos_all,
    charge_all,
    grad_all,
    outgoing,
    extended,
    returning,
    returned,
    pair_total,
    pairs,
    filt,
    structure,
    wave_rows,
    wave_columns,
    table,
    own_table,
    field,
    half_out,
    half_in,
    sums,
    slots,
    reduced,
    owned,
    gather_send,
    gather_recv,
    pass_send,
    pass_recv,
    side_send,
    side_recv,
    half_send,
    half_recv,
    weight_send,
    weight_recv,
    load,
):
    (
        feats,
        positions,
        species,
        waves,
        smearing,
        species_gain,
        w_charge,
        w_message,
        w_radial,
        w_out,
        senders,
        receivers,
        mask,
        lengths,
        ghost_down,
        ghost_up,
        cotangent,
    ) = staged
    atoms = feats.shape[1]
    ghosts = ghost_down.shape[1]
    bases = w_radial.shape[0]
    wave_count = waves.shape[1]
    half = wave_count // 2
    chips = domains // 2
    devices = domains * cells
    inv_waves = 1.0 / math.sqrt(wave_count)
    inv_atoms = 1.0 / math.sqrt(atoms * domains)
    grad_scale = 1.0 / math.sqrt(cells * atoms * domains)

    cell = lax.axis_index("cell")
    me = lax.axis_index("dom")
    core = lax.rem(me, 2)
    chip = lax.div(me, 2)
    partner = me + 1 - 2 * core
    linear = cell * domains + me

    def place(index):
        return (lax.div(index, domains), lax.rem(index, domains))

    loads = [
        pltpu.make_async_copy(source, target, load.at[index])
        for index, (source, target) in enumerate(zip(sources, staged))
    ]
    for copy in loads:
        copy.start()

    barrier = pltpu.get_barrier_semaphore()

    def greet(step, carry):
        target = lax.rem(linear + step, devices)
        pl.semaphore_signal(barrier, inc=1, device_id=place(target), device_id_type=MESH)
        return carry

    lax.fori_loop(1, devices, greet, 0, unroll=devices <= 32)

    def remote(source, target, send, recv, index):
        return pltpu.make_async_remote_copy(
            src_ref=source,
            dst_ref=target,
            send_sem=send,
            recv_sem=recv,
            device_id=(cell, index),
            device_id_type=MESH,
        )

    pair_total[...] = jnp.zeros_like(pair_total)

    def edge_step(step, carry):
        at = pl.ds(pl.multiple_of(step * edge_chunk, edge_chunk), edge_chunk)
        weights = edge_weights(lengths[:, at], mask[:, at], bases)
        receiver = spread(receivers[:, at], atoms).astype(jnp.bfloat16)
        sender = spread(senders[:, at], atoms + 2 * ghosts).astype(jnp.bfloat16)
        left = jnp.concatenate([receiver * weights[b : b + 1] for b in range(bases)], axis=0)
        pair_total[...] += by_transpose(left, sender)
        return carry

    for index in (0, 1, 2, 3, 4, 5, 6, 7, 8, 9, 14, 15, 16):
        loads[index].wait()
    rows = feats[0]
    upstream_cot = cotangent[0]
    pos_all[me] = jnp.zeros(pos_all.shape[1:], jnp.float32)
    pos_all[me, 0:3, :] = positions[:, 0, :]
    kinds = spread(species[...], species_gain.shape[0]).astype(jnp.float32)
    gain = dot(kinds, species_gain[...], ((0,), (0,)), lax.Precision.HIGHEST)
    charge_all[me] = (plain(rows, w_charge[...]) * gain).astype(jnp.bfloat16)
    down_spread = spread(ghost_down[...], atoms).astype(jnp.bfloat16)
    up_spread = spread(ghost_up[...], atoms).astype(jnp.bfloat16)
    outgoing[0] = rows_by_rows(up_spread, rows).astype(jnp.bfloat16)
    outgoing[1] = rows_by_rows(down_spread, rows).astype(jnp.bfloat16)
    extended[0:atoms, :] = rows

    pl.semaphore_wait(barrier, devices - 1)

    def gather_copy(buffer, which, step, index):
        return remote(
            buffer.at[index],
            buffer.at[index],
            gather_send.at[which, step],
            gather_recv.at[which, step],
            lax.rem(chip + step, chips) * 2 + core,
        )

    def pass_copy(buffer, which, step, index):
        return remote(
            buffer.at[index],
            buffer.at[index],
            pass_send.at[which, step],
            pass_recv.at[which, step],
            partner,
        )

    def gather_start(buffer, which):
        pass_copy(buffer, which, 0, me).start()
        for step in range(1, chips):
            gather_copy(buffer, which, step, me).start()

    def chip_at(step):
        return lax.rem(chip - step + chips, chips)

    def gather_pass(buffer, which, step):
        source = chip_at(step) * 2 + core
        gather_copy(buffer, which, step, source).wait_recv()
        pass_copy(buffer, which, step, source).start()

    def gather_wait(buffer, which, step):
        pass_copy(buffer, which, step, chip_at(step) * 2 + (1 - core)).wait_recv()

    def gather_end(buffer, which):
        for step in range(1, chips):
            gather_copy(buffer, which, step, me).wait_send()
        for step in range(chips):
            pass_copy(buffer, which, step, me).wait_send()

    gather_start(pos_all, 0)
    gather_start(charge_all, 1)
    above = lax.rem(me + 1, domains)
    below = lax.rem(me + domains - 1, domains)
    low = pl.ds(atoms, ghosts)
    high = pl.ds(atoms + ghosts, ghosts)
    ghost_copies = [
        remote(outgoing.at[0], extended.at[low], side_send.at[0], side_recv.at[0], above),
        remote(outgoing.at[1], extended.at[high], side_send.at[1], side_recv.at[1], below),
    ]
    for copy in ghost_copies:
        copy.start()

    for index in (10, 11, 12, 13):
        loads[index].wait()
    edge_steps = lengths.shape[1] // edge_chunk
    alone = edge_steps // 3
    lax.fori_loop(0, alone, edge_step, 0)

    wave_rows[...] = jnp.zeros_like(wave_rows)
    wave_rows[0:3, :] = waves[:, pl.ds(pl.multiple_of(core * half, lane), half)].astype(jnp.float32)
    ones = jnp.ones((coord_rows, lane), jnp.bfloat16)
    wave = wave_rows[...]
    squared = rows_by_rows((wave * wave).astype(jnp.bfloat16), ones)
    filt[...] = filter_factor * jnp.exp(-squared * smearing[...]) * lax.rsqrt(squared)
    wave_columns[...] = jnp.concatenate([wave, wave, wave], axis=0).T.astype(jnp.bfloat16)
    pair = 2 * atoms

    def pair_of(step):
        return pl.ds(chip_at(step) * 2, 2)

    def columns(step):
        return pl.ds(pl.multiple_of(step * pair, lane), pair)

    def table_block(step):
        block = pos_all[pair_of(step)]
        exact = jnp.concatenate([block[0], block[1]], axis=1)
        first = exact.astype(jnp.bfloat16).astype(jnp.float32)
        rest = exact - first
        second = rest.astype(jnp.bfloat16).astype(jnp.float32)
        points = jnp.concatenate([first, second, rest - second], axis=0).astype(jnp.bfloat16)
        at = columns(step)
        for low_row in range(0, half, wave_chunk):
            piece = slice(low_row, low_row + wave_chunk)
            turns = plain(wave_columns[piece, :], points)
            turns = turns - jnp.floor(turns + 0.5)
            square = turns * turns
            table[piece, at] = horner(cosine_terms, square).astype(jnp.bfloat16)
            table[half + low_row : half + low_row + wave_chunk, at] = (
                turns * horner(sine_terms, square)
            ).astype(jnp.bfloat16)

    shared = edge_steps - alone
    blocks = chips // shared
    assert blocks * shared == chips
    for step in range(1, chips):
        gather_pass(pos_all, 0, step)

    def shared_step(step, carry):
        @pl.when(step == shared // 4)
        def _():
            for back in range(1, chips):
                gather_pass(charge_all, 1, back)

        for block in range(blocks):
            gather_wait(pos_all, 0, step * blocks + block)
        edge_step(alone + step, carry)
        for block in range(blocks):
            table_block(step * blocks + block)
        return carry

    lax.fori_loop(0, shared, shared_step, 0)
    pairs[...] = pair_total[...].astype(jnp.bfloat16)

    size = 2

    def structure_sums(buffer, which, passing):
        structure[...] = jnp.zeros_like(structure)

        def group_step(group, carry):
            if passing:
                for j in range(size):
                    later = (group + 1) * size + j

                    @pl.when(later < chips)
                    def _():
                        gather_pass(buffer, which, later)

            for j in range(size):
                gather_wait(buffer, which, group * size + j)
            block = jnp.concatenate(
                [buffer[chip_at(group * size + j) * 2 + c] for j in range(size) for c in (0, 1)]
            )
            wide = size * pair
            at = pl.ds(pl.multiple_of(group * wide, lane), wide)
            structure[...] += plain(table[:, at], block)
            return carry

        lax.fori_loop(0, chips // size, group_step, 0)

    structure_sums(charge_all, 1, False)
    own_table[...] = table[:, 0:pair].T

    def fill_field(scale):
        scaled = filt[...] * scale
        field[0:half, :] = (scaled * structure[0:half, :]).astype(jnp.bfloat16)
        field[half:, :] = (scaled * structure[half:, :]).astype(jnp.bfloat16)

    fill_field(inv_atoms)
    gather_end(pos_all, 0)
    gather_end(charge_all, 1)

    def exchange(which):
        partial = plain(own_table[...], field[...])
        half_out[which] = partial.reshape(2, atoms, -1)
        copy = remote(
            half_out.at[which, 1 - core],
            half_in.at[which],
            half_send.at[which],
            half_recv.at[which],
            partner,
        )
        copy.start()
        return copy

    first_exchange = exchange(0)
    for copy in ghost_copies:
        copy.wait()
    message_rows = plain(extended[...], w_message[...]).astype(jnp.bfloat16)
    mixed = plain(pairs[...], message_rows).reshape(bases, atoms, -1)
    aggregate = jnp.zeros((atoms, rows.shape[1]), jnp.float32)
    for b in range(bases):
        aggregate += w_radial[b : b + 1, :] * mixed[b]
    grad_act = by_transpose(upstream_cot, w_out[...])
    first_exchange.wait()
    potential = (half_out[0, core] + half_in[0]) * inv_waves
    preact = aggregate * edge_scale + potential
    sig = 1.0 / (1.0 + jnp.exp(-preact))
    grad_pre = grad_act * sig * (1.0 + preact * (1.0 - sig))
    grad_all[me] = grad_pre.astype(jnp.bfloat16)
    gather_start(grad_all, 2)

    act = (preact * sig).astype(jnp.bfloat16)
    updated_ref[0] = (rows.astype(jnp.float32) + plain(act, w_out[...])).astype(jnp.bfloat16)
    scaled_pre = edge_scale * grad_pre
    weighted = jnp.concatenate(
        [(w_radial[b : b + 1, :] * scaled_pre).astype(jnp.bfloat16) for b in range(bases)], axis=0
    )
    grad_msg = rows_by_rows(pairs[...], weighted).astype(jnp.bfloat16)
    grad_rows = by_transpose(grad_msg, w_message[...])
    returning[...] = grad_rows[atoms:].reshape(returning.shape)
    return_copies = [
        remote(returning.at[0], returned.at[0], side_send.at[2], side_recv.at[2], below),
        remote(returning.at[1], returned.at[1], side_send.at[3], side_recv.at[3], above),
    ]
    for copy in return_copies:
        copy.start()
    width = rows.shape[1]
    sums[0:width, :] = rows_by_rows(extended[...], grad_msg).astype(jnp.bfloat16)
    sums[width : 2 * width, :] = rows_by_rows(act, upstream_cot).astype(jnp.bfloat16)
    grad_radial = [jnp.sum(mixed[b] * scaled_pre, axis=0, keepdims=True) for b in range(bases)]
    grad_radial.append(jnp.zeros((part_rows - bases, width), jnp.float32))
    sums[3 * width :, :] = jnp.concatenate(grad_radial, axis=0).astype(jnp.bfloat16)

    owners = sums.shape[0] // part_rows
    early = 2 * width // part_rows

    def part(ref, owner):
        return ref.at[pl.ds(pl.multiple_of(owner * part_rows, part_rows), part_rows)]

    def send_part(owner):
        return pltpu.make_async_remote_copy(
            src_ref=part(sums, owner),
            dst_ref=slots.at[linear],
            send_sem=weight_send.at[0],
            recv_sem=weight_recv.at[0],
            device_id=place(owner),
            device_id_type=MESH,
        )

    def scatter_start(first, last):
        for owner in range(first, last):

            @pl.when(linear != owner)
            def _():
                send_part(owner).start()

    def wait_bytes(ref, which):
        return pltpu.make_async_remote_copy(
            src_ref=ref,
            dst_ref=ref,
            send_sem=weight_send.at[which],
            recv_sem=weight_recv.at[which],
            device_id=(cell, partner),
            device_id_type=MESH,
        )

    def share():
        @pl.when(linear < owners)
        def _():
            wait_bytes(slots.at[pl.ds(0, devices - 1)], 0).wait_recv()
            slots[linear] = part(sums, linear)[...]
            total = slots[0].astype(jnp.float32)
            for index in range(1, devices):
                total += slots[index].astype(jnp.float32)
            owned[...] = (total * grad_scale).astype(jnp.bfloat16)

            def send(step, carry):
                pltpu.make_async_remote_copy(
                    src_ref=owned,
                    dst_ref=part(reduced, linear),
                    send_sem=weight_send.at[1],
                    recv_sem=weight_recv.at[1],
                    device_id=place(lax.rem(linear + step, devices)),
                    device_id_type=MESH,
                ).start()
                return carry

            lax.fori_loop(1, devices, send, 0, unroll=devices <= 32)
            part(reduced, linear)[...] = owned[...]

    def share_end():
        @pl.when(linear < owners)
        def _():
            wait_bytes(reduced.at[pl.ds(0, (owners - 1) * part_rows)], 1).wait_recv()
            wait_bytes(slots.at[pl.ds(0, devices - 1)], 1).wait_send()
            wait_bytes(sums.at[pl.ds(0, (owners - 1) * part_rows)], 0).wait_send()

        @pl.when(linear >= owners)
        def _():
            wait_bytes(reduced, 1).wait_recv()
            wait_bytes(sums, 0).wait_send()

    for step in range(1, size):
        gather_pass(grad_all, 2, step)
    structure_sums(grad_all, 2, True)
    fill_field(inv_waves * inv_atoms)
    gather_end(grad_all, 2)
    second_exchange = exchange(1)

    scatter_start(0, early)
    second_exchange.wait()
    grad_raw = ((half_out[1, core] + half_in[1]) * gain).astype(jnp.bfloat16)
    sums[2 * width : 3 * width, :] = rows_by_rows(rows, grad_raw).astype(jnp.bfloat16)
    scatter_start(early, owners)
    for copy in return_copies:
        copy.wait()
    total = (
        upstream_cot.astype(jnp.float32)
        + by_transpose(grad_raw, w_charge[...])
        + grad_rows[:atoms]
        + dot(down_spread.astype(jnp.float32), returned[1], ((1,), (0,)), lax.Precision.HIGHEST)
        + dot(up_spread.astype(jnp.float32), returned[0], ((1,), (0,)), lax.Precision.HIGHEST)
    )
    feat_grad_ref[0] = total.astype(jnp.bfloat16)

    share()
    share_end()
    final = reduced[...].astype(jnp.float32)
    grad_message_ref[...] = final[0:width]
    grad_out_ref[...] = final[width : 2 * width]
    grad_charge_ref[...] = final[2 * width : 3 * width]
    grad_radial_ref[...] = final[3 * width : 3 * width + bases]


def write_kernel(*refs):
    count = len(refs) // 3
    sources, results, held, done = refs[:count], refs[count : 2 * count], refs[2 * count : -1], refs[-1]
    first = [
        pltpu.make_async_copy(sources[index], held[index], done.at[0, index])
        for index in range(count)
    ]
    second = [
        pltpu.make_async_copy(held[index], results[index], done.at[1, index])
        for index in range(count)
    ]
    for copy in first:
        copy.start()
    for copy, onward in zip(first, second):
        copy.wait()
        onward.start()
    for copy in second:
        copy.wait()


def per_device(
    feats,
    positions,
    species,
    wave_vectors,
    smearing,
    species_gain,
    w_charge,
    w_message,
    w_radial,
    w_out,
    edge_sender,
    edge_receiver,
    edge_mask,
    edge_length,
    ghost_down,
    ghost_up,
    cotangent,
):
    domains = lax.axis_size("dom")
    cells = lax.axis_size("cell")
    atoms, width = feats.shape[1:]
    ghosts = ghost_down.shape[1]
    bases = w_radial.shape[0]
    wave_count = wave_vectors.shape[1]
    devices = domains * cells
    chips = domains // 2
    f32, bf16 = jnp.float32, jnp.bfloat16
    vmem = pl.BlockSpec(memory_space=pltpu.VMEM)
    count = 3 * width + part_rows
    scratch = [
        pltpu.VMEM((domains, coord_rows, atoms), f32),
        pltpu.VMEM((domains, atoms, width), bf16),
        pltpu.VMEM((domains, atoms, width), bf16),
        pltpu.VMEM((2, ghosts, width), bf16),
        pltpu.VMEM((atoms + 2 * ghosts, width), bf16),
        pltpu.VMEM((2, ghosts, width), f32),
        pltpu.VMEM((2, ghosts, width), f32),
        pltpu.VMEM((bases * atoms, atoms + 2 * ghosts), f32),
        pltpu.VMEM((bases * atoms, atoms + 2 * ghosts), bf16),
        pltpu.VMEM((wave_count // 2, width), f32),
        pltpu.VMEM((wave_count, width), f32),
        pltpu.VMEM((coord_rows, wave_count // 2), f32),
        pltpu.VMEM((wave_count // 2, 3 * coord_rows), bf16),
        pltpu.VMEM((wave_count, domains * atoms), bf16),
        pltpu.VMEM((2 * atoms, wave_count), bf16),
        pltpu.VMEM((wave_count, width), bf16),
        pltpu.VMEM((2, 2, atoms, width), f32),
        pltpu.VMEM((2, atoms, width), f32),
        pltpu.VMEM((count, width), bf16),
        pltpu.VMEM((devices, part_rows, width), bf16),
        pltpu.VMEM((count, width), bf16),
        pltpu.VMEM((part_rows, width), bf16),
        pltpu.SemaphoreType.DMA((3, chips)),
        pltpu.SemaphoreType.DMA((3, chips)),
        pltpu.SemaphoreType.DMA((3, chips)),
        pltpu.SemaphoreType.DMA((3, chips)),
        pltpu.SemaphoreType.DMA((4,)),
        pltpu.SemaphoreType.DMA((4,)),
        pltpu.SemaphoreType.DMA((2,)),
        pltpu.SemaphoreType.DMA((2,)),
        pltpu.SemaphoreType.DMA((2,)),
        pltpu.SemaphoreType.DMA((2,)),
    ]
    shape = jax.ShapeDtypeStruct
    operands = (
        feats,
        positions.transpose(1, 0, 2),
        species,
        wave_vectors,
        smearing[None, :],
        species_gain,
        w_charge,
        w_message,
        w_radial,
        w_out,
        edge_sender,
        edge_receiver,
        edge_mask,
        edge_length,
        ghost_down,
        ghost_up,
        cotangent,
    )
    count = len(operands)
    staged = [pltpu.VMEM(value.shape, value.dtype) for value in operands]
    scratch = [*staged, *scratch, pltpu.SemaphoreType.DMA((count,))]
    outs = (
        shape(feats.shape, bf16),
        shape(feats.shape, bf16),
        shape((width, width), f32),
        shape((width, width), f32),
        shape((bases, width), f32),
        shape((width, width), f32),
    )

    def body(*refs):
        sources, rest = refs[:count], refs[count:]
        results, rest = rest[: len(outs)], rest[len(outs) :]
        block_kernel(domains, cells, sources, rest[:count], *results, *rest[count:])

    results = pl.pallas_call(
        body,
        out_shape=outs,
        in_specs=[pl.BlockSpec(memory_space=pltpu.HBM)] * count,
        out_specs=(vmem,) * len(outs),
        scratch_shapes=scratch,
        compiler_params=pltpu.CompilerParams(
            collective_id=0, has_side_effects=True, vmem_limit_bytes=64 * 1024 * 1024
        ),
        name="ewald_block",
    )(*operands)
    return pl.pallas_call(
        write_kernel,
        out_shape=outs,
        in_specs=[pl.BlockSpec(memory_space=pltpu.HBM)] * len(outs),
        out_specs=(pl.BlockSpec(memory_space=pltpu.HBM),) * len(outs),
        scratch_shapes=[
            *[pltpu.VMEM(out.shape, out.dtype) for out in outs],
            pltpu.SemaphoreType.DMA((2, len(outs))),
        ],
        compiler_params=pltpu.CompilerParams(vmem_limit_bytes=64 * 1024 * 1024),
        name="write_out",
    )(*results)


def solution(mesh):
    placed = (
        P("cell", "dom", None),
        P("cell", None, "dom"),
        P("cell", "dom"),
        P(),
        P(),
        P(),
        P(),
        P(),
        P(),
        P(),
        P("cell", "dom"),
        P("cell", "dom"),
        P("cell", "dom"),
        P("cell", "dom"),
        P("cell", "dom"),
        P("cell", "dom"),
        P("cell", "dom", None),
    )
    return jax.shard_map(
        per_device,
        mesh=mesh,
        in_specs=placed,
        out_specs=(P("cell", "dom", None), P("cell", "dom", None), P(), P(), P(), P()),
        check_vma=False,
    )
```

```python
import math

import jax
import jax.numpy as jnp
from jax import lax
from jax.experimental import pallas as pl
from jax.experimental.pallas import tpu as pltpu
from jax.sharding import PartitionSpec as P

cutoff_radius = 6.0
basis_width = 0.75
edge_scale = 0.25
filter_factor = 12.0
MESH = pl.DeviceIdType.MESH
edge_chunk = 1024
wave_chunk = 128
lane = 128
part_rows = 16
coord_rows = 8

sine_terms = (-0.784374028, 3.59478808, -7.30744342, 4.4428679)
cosine_terms = (-1.72834866, 5.7152384, -6.97764206, 1.41420408)


def horner(terms, x):
    value = terms[0] * x + terms[1]
    for term in terms[2:]:
        value = value * x + term
    return value


def dot(left, right, dims, precision=None):
    return lax.dot_general(
        left, right, (dims, ((), ())), preferred_element_type=jnp.float32, precision=precision
    )


def rows_by_rows(left, right):
    return dot(left, right, ((0,), (0,)))


def plain(left, right):
    return dot(left, right, ((1,), (0,)))


def by_transpose(left, right):
    return dot(left, right, ((1,), (1,)))


def edge_weights(length, mask, bases):
    shape = (bases, length.shape[1])
    centers = 0.5 + basis_width * lax.broadcasted_iota(jnp.int32, shape, 0).astype(jnp.float32)
    basis = jnp.exp(-jnp.square((length - centers) / basis_width))
    turn = math.pi * (length / cutoff_radius - 0.5)
    square = turn * turn
    sine = turn * horner(
        (-1.0 / 39916800.0, 1.0 / 362880.0, -1.0 / 5040.0, 1.0 / 120.0, -1.0 / 6.0, 1.0), square
    )
    return (basis * (0.5 * (1.0 - sine) * mask.astype(jnp.float32))).astype(jnp.bfloat16)


def spread(index, rows):
    shape = (rows, index.shape[1])
    return lax.broadcasted_iota(jnp.int32, shape, 0) == index


def block_kernel(
    domains,
    cells,
    sources,
    staged,
    updated_ref,
    feat_grad_ref,
    grad_charge_ref,
    grad_message_ref,
    grad_radial_ref,
    grad_out_ref,
    pos_all,
    charge_all,
    grad_all,
    outgoing,
    extended,
    returning,
    returned,
    pair_total,
    pairs,
    filt,
    structure,
    wave_rows,
    wave_columns,
    table,
    own_table,
    field,
    half_out,
    half_in,
    sums,
    slots,
    reduced,
    owned,
    gather_send,
    gather_recv,
    pass_send,
    pass_recv,
    side_send,
    side_recv,
    half_send,
    half_recv,
    weight_send,
    weight_recv,
    load,
):
    (
        feats,
        positions,
        species,
        waves,
        smearing,
        species_gain,
        w_charge,
        w_message,
        w_radial,
        w_out,
        senders,
        receivers,
        mask,
        lengths,
        ghost_down,
        ghost_up,
        cotangent,
    ) = staged
    atoms = feats.shape[1]
    ghosts = ghost_down.shape[1]
    bases = w_radial.shape[0]
    wave_count = waves.shape[1]
    half = wave_count // 2
    chips = domains // 2
    devices = domains * cells
    inv_waves = 1.0 / math.sqrt(wave_count)
    inv_atoms = 1.0 / math.sqrt(atoms * domains)
    grad_scale = 1.0 / math.sqrt(cells * atoms * domains)

    cell = lax.axis_index("cell")
    me = lax.axis_index("dom")
    core = lax.rem(me, 2)
    chip = lax.div(me, 2)
    partner = me + 1 - 2 * core
    linear = cell * domains + me

    def place(index):
        return (lax.div(index, domains), lax.rem(index, domains))

    loads = [
        pltpu.make_async_copy(source, target, load.at[index])
        for index, (source, target) in enumerate(zip(sources, staged))
    ]
    for copy in loads:
        copy.start()

    barrier = pltpu.get_barrier_semaphore()

    def greet(step, carry):
        target = lax.rem(linear + step, devices)
        pl.semaphore_signal(barrier, inc=1, device_id=place(target), device_id_type=MESH)
        return carry

    lax.fori_loop(1, devices, greet, 0, unroll=devices <= 32)

    def remote(source, target, send, recv, index):
        return pltpu.make_async_remote_copy(
            src_ref=source,
            dst_ref=target,
            send_sem=send,
            recv_sem=recv,
            device_id=(cell, index),
            device_id_type=MESH,
        )


    def edge_step(step, carry):
        at = pl.ds(pl.multiple_of(step * edge_chunk, edge_chunk), edge_chunk)
        weights = edge_weights(lengths[:, at], mask[:, at], bases)
        receiver = spread(receivers[:, at], atoms).astype(jnp.bfloat16)
        sender = spread(senders[:, at], atoms + 2 * ghosts).astype(jnp.bfloat16)
        left = jnp.concatenate([receiver * weights[b : b + 1] for b in range(bases)], axis=0)
        pair_total[...] += by_transpose(left, sender)
        return carry

    for index in (0, 1, 2, 3, 4, 5, 6, 7, 8, 9, 14, 15, 16):
        loads[index].wait()
    rows = feats[0]
    upstream_cot = cotangent[0]
    pos_all[me] = jnp.zeros(pos_all.shape[1:], jnp.float32)
    pos_all[me, 0:3, :] = positions[:, 0, :]
    kinds = spread(species[...], species_gain.shape[0]).astype(jnp.float32)
    gain = dot(kinds, species_gain[...], ((0,), (0,)), lax.Precision.HIGHEST)
    charge_all[me] = (plain(rows, w_charge[...]) * gain).astype(jnp.bfloat16)
    down_spread = spread(ghost_down[...], atoms).astype(jnp.bfloat16)
    up_spread = spread(ghost_up[...], atoms).astype(jnp.bfloat16)
    outgoing[0] = rows_by_rows(up_spread, rows).astype(jnp.bfloat16)
    outgoing[1] = rows_by_rows(down_spread, rows).astype(jnp.bfloat16)
    extended[0:atoms, :] = rows

    wave_rows[...] = jnp.zeros_like(wave_rows)
    wave_rows[0:3, :] = waves[:, pl.ds(pl.multiple_of(core * half, lane), half)].astype(jnp.float32)
    ones = jnp.ones((coord_rows, lane), jnp.bfloat16)
    wave = wave_rows[...]
    squared = rows_by_rows((wave * wave).astype(jnp.bfloat16), ones)
    filt[...] = filter_factor * jnp.exp(-squared * smearing[...]) * lax.rsqrt(squared)
    wave_columns[...] = jnp.concatenate([wave, wave, wave], axis=0).T.astype(jnp.bfloat16)
    pair_total[...] = jnp.zeros_like(pair_total)

    pl.semaphore_wait(barrier, devices - 1)

    def gather_copy(buffer, which, step, index):
        return remote(
            buffer.at[index],
            buffer.at[index],
            gather_send.at[which, step],
            gather_recv.at[which, step],
            lax.rem(chip + step, chips) * 2 + core,
        )

    def pass_copy(buffer, which, step, index):
        return remote(
            buffer.at[index],
            buffer.at[index],
            pass_send.at[which, step],
            pass_recv.at[which, step],
            partner,
        )

    def gather_start(buffer, which):
        pass_copy(buffer, which, 0, me).start()
        for step in range(1, chips):
            gather_copy(buffer, which, step, me).start()

    def chip_at(step):
        return lax.rem(chip - step + chips, chips)

    def gather_pass(buffer, which, step):
        source = chip_at(step) * 2 + core
        gather_copy(buffer, which, step, source).wait_recv()
        pass_copy(buffer, which, step, source).start()

    def gather_wait(buffer, which, step):
        pass_copy(buffer, which, step, chip_at(step) * 2 + (1 - core)).wait_recv()

    def gather_end(buffer, which):
        for step in range(1, chips):
            gather_copy(buffer, which, step, me).wait_send()
        for step in range(chips):
            pass_copy(buffer, which, step, me).wait_send()

    gather_start(pos_all, 0)
    gather_start(charge_all, 1)
    above = lax.rem(me + 1, domains)
    below = lax.rem(me + domains - 1, domains)
    low = pl.ds(atoms, ghosts)
    high = pl.ds(atoms + ghosts, ghosts)
    ghost_copies = [
        remote(outgoing.at[0], extended.at[low], side_send.at[0], side_recv.at[0], above),
        remote(outgoing.at[1], extended.at[high], side_send.at[1], side_recv.at[1], below),
    ]
    for copy in ghost_copies:
        copy.start()

    for index in (10, 11, 12, 13):
        loads[index].wait()
    edge_steps = lengths.shape[1] // edge_chunk
    alone = edge_steps // 3
    lax.fori_loop(0, alone, edge_step, 0)

    pair = 2 * atoms

    def pair_of(step):
        return pl.ds(chip_at(step) * 2, 2)

    def columns(step):
        return pl.ds(pl.multiple_of(step * pair, lane), pair)

    def table_block(step):
        block = pos_all[pair_of(step)]
        exact = jnp.concatenate([block[0], block[1]], axis=1)
        first = exact.astype(jnp.bfloat16).astype(jnp.float32)
        rest = exact - first
        second = rest.astype(jnp.bfloat16).astype(jnp.float32)
        points = jnp.concatenate([first, second, rest - second], axis=0).astype(jnp.bfloat16)
        at = columns(step)
        for low_row in range(0, half, wave_chunk):
            piece = slice(low_row, low_row + wave_chunk)
            turns = plain(wave_columns[piece, :], points)
            turns = turns - jnp.floor(turns + 0.5)
            square = turns * turns
            sine = turns * horner(sine_terms, square)
            table[piece, at] = (1.0 - sine * sine).astype(jnp.bfloat16)
            table[half + low_row : half + low_row + wave_chunk, at] = (
                sine * horner(cosine_terms, square)
            ).astype(jnp.bfloat16)

    shared = edge_steps - alone
    blocks = chips // shared
    assert blocks * shared == chips
    for step in range(1, chips):
        gather_pass(pos_all, 0, step)

    def shared_step(step, carry):
        @pl.when(step == shared // 4)
        def _():
            for back in range(1, chips):
                gather_pass(charge_all, 1, back)

        for block in range(blocks):
            gather_wait(pos_all, 0, step * blocks + block)
        edge_step(alone + step, carry)
        for block in range(blocks):
            table_block(step * blocks + block)
        return carry

    lax.fori_loop(0, shared, shared_step, 0)
    pairs[...] = pair_total[...].astype(jnp.bfloat16)

    size = 2

    def structure_sums(buffer, which, passing):
        structure[...] = jnp.zeros_like(structure)

        def group_step(group, carry):
            if passing:
                for j in range(size):
                    later = (group + 1) * size + j

                    @pl.when(later < chips)
                    def _():
                        gather_pass(buffer, which, later)

            for j in range(size):
                gather_wait(buffer, which, group * size + j)
            block = jnp.concatenate(
                [buffer[chip_at(group * size + j) * 2 + c] for j in range(size) for c in (0, 1)]
            )
            wide = size * pair
            at = pl.ds(pl.multiple_of(group * wide, lane), wide)
            structure[...] += plain(table[:, at], block)
            return carry

        lax.fori_loop(0, chips // size, group_step, 0)

    structure_sums(charge_all, 1, False)
    own_table[...] = table[:, 0:pair].T

    def fill_field(scale):
        scaled = filt[...] * scale
        field[0:half, :] = (scaled * structure[0:half, :]).astype(jnp.bfloat16)
        field[half:, :] = (scaled * structure[half:, :]).astype(jnp.bfloat16)

    fill_field(inv_atoms)
    gather_end(pos_all, 0)
    gather_end(charge_all, 1)

    def exchange(which):
        partial = plain(own_table[...], field[...])
        half_out[which] = partial.reshape(2, atoms, -1)
        copy = remote(
            half_out.at[which, 1 - core],
            half_in.at[which],
            half_send.at[which],
            half_recv.at[which],
            partner,
        )
        copy.start()
        return copy

    first_exchange = exchange(0)
    for copy in ghost_copies:
        copy.wait()
    message_rows = plain(extended[...], w_message[...]).astype(jnp.bfloat16)
    mixed = plain(pairs[...], message_rows).reshape(bases, atoms, -1)
    aggregate = jnp.zeros((atoms, rows.shape[1]), jnp.float32)
    for b in range(bases):
        aggregate += w_radial[b : b + 1, :] * mixed[b]
    grad_act = by_transpose(upstream_cot, w_out[...])
    first_exchange.wait()
    potential = (half_out[0, core] + half_in[0]) * inv_waves
    preact = aggregate * edge_scale + potential
    sig = 1.0 / (1.0 + jnp.exp(-preact))
    grad_pre = grad_act * sig * (1.0 + preact * (1.0 - sig))
    grad_all[me] = grad_pre.astype(jnp.bfloat16)
    gather_start(grad_all, 2)

    act = (preact * sig).astype(jnp.bfloat16)
    updated_ref[0] = (rows.astype(jnp.float32) + plain(act, w_out[...])).astype(jnp.bfloat16)
    scaled_pre = edge_scale * grad_pre
    weighted = jnp.concatenate(
        [(w_radial[b : b + 1, :] * scaled_pre).astype(jnp.bfloat16) for b in range(bases)], axis=0
    )
    grad_msg = rows_by_rows(pairs[...], weighted).astype(jnp.bfloat16)
    grad_rows = by_transpose(grad_msg, w_message[...])
    returning[...] = grad_rows[atoms:].reshape(returning.shape)
    return_copies = [
        remote(returning.at[0], returned.at[0], side_send.at[2], side_recv.at[2], below),
        remote(returning.at[1], returned.at[1], side_send.at[3], side_recv.at[3], above),
    ]
    for copy in return_copies:
        copy.start()
    width = rows.shape[1]
    sums[0:width, :] = rows_by_rows(extended[...], grad_msg).astype(jnp.bfloat16)
    sums[width : 2 * width, :] = rows_by_rows(act, upstream_cot).astype(jnp.bfloat16)
    grad_radial = [jnp.sum(mixed[b] * scaled_pre, axis=0, keepdims=True) for b in range(bases)]
    grad_radial.append(jnp.zeros((part_rows - bases, width), jnp.float32))
    sums[3 * width :, :] = jnp.concatenate(grad_radial, axis=0).astype(jnp.bfloat16)

    owners = sums.shape[0] // part_rows
    early = 2 * width // part_rows

    def part(ref, owner):
        return ref.at[pl.ds(pl.multiple_of(owner * part_rows, part_rows), part_rows)]

    def send_part(owner):
        return pltpu.make_async_remote_copy(
            src_ref=part(sums, owner),
            dst_ref=slots.at[linear],
            send_sem=weight_send.at[0],
            recv_sem=weight_recv.at[0],
            device_id=place(owner),
            device_id_type=MESH,
        )

    def scatter_start(first, last):
        for owner in range(first, last):

            @pl.when(linear != owner)
            def _():
                send_part(owner).start()

    def wait_bytes(ref, which):
        return pltpu.make_async_remote_copy(
            src_ref=ref,
            dst_ref=ref,
            send_sem=weight_send.at[which],
            recv_sem=weight_recv.at[which],
            device_id=(cell, partner),
            device_id_type=MESH,
        )

    def share():
        @pl.when(linear < owners)
        def _():
            wait_bytes(slots.at[pl.ds(0, devices - 1)], 0).wait_recv()
            slots[linear] = part(sums, linear)[...]
            total = slots[0].astype(jnp.float32)
            for index in range(1, devices):
                total += slots[index].astype(jnp.float32)
            owned[...] = (total * grad_scale).astype(jnp.bfloat16)

            def send(step, carry):
                pltpu.make_async_remote_copy(
                    src_ref=owned,
                    dst_ref=part(reduced, linear),
                    send_sem=weight_send.at[1],
                    recv_sem=weight_recv.at[1],
                    device_id=place(lax.rem(linear + step, devices)),
                    device_id_type=MESH,
                ).start()
                return carry

            lax.fori_loop(1, devices, send, 0, unroll=devices <= 32)
            part(reduced, linear)[...] = owned[...]

    def share_end():
        @pl.when(linear < owners)
        def _():
            wait_bytes(reduced.at[pl.ds(0, (owners - 1) * part_rows)], 1).wait_recv()
            wait_bytes(slots.at[pl.ds(0, devices - 1)], 1).wait_send()
            wait_bytes(sums.at[pl.ds(0, (owners - 1) * part_rows)], 0).wait_send()

        @pl.when(linear >= owners)
        def _():
            wait_bytes(reduced, 1).wait_recv()
            wait_bytes(sums, 0).wait_send()

    for step in range(1, size):
        gather_pass(grad_all, 2, step)
    structure_sums(grad_all, 2, True)
    fill_field(inv_waves * inv_atoms)
    gather_end(grad_all, 2)
    second_exchange = exchange(1)

    scatter_start(0, early)
    second_exchange.wait()
    grad_raw = ((half_out[1, core] + half_in[1]) * gain).astype(jnp.bfloat16)
    sums[2 * width : 3 * width, :] = rows_by_rows(rows, grad_raw).astype(jnp.bfloat16)
    scatter_start(early, owners)
    for copy in return_copies:
        copy.wait()
    total = (
        upstream_cot.astype(jnp.float32)
        + by_transpose(grad_raw, w_charge[...])
        + grad_rows[:atoms]
        + dot(down_spread.astype(jnp.float32), returned[1], ((1,), (0,)), lax.Precision.HIGHEST)
        + dot(up_spread.astype(jnp.float32), returned[0], ((1,), (0,)), lax.Precision.HIGHEST)
    )
    feat_grad_ref[0] = total.astype(jnp.bfloat16)

    share()
    share_end()
    final = reduced[...].astype(jnp.float32)
    grad_message_ref[...] = final[0:width]
    grad_out_ref[...] = final[width : 2 * width]
    grad_charge_ref[...] = final[2 * width : 3 * width]
    grad_radial_ref[...] = final[3 * width : 3 * width + bases]


def write_kernel(*refs):
    count = len(refs) // 3
    sources, results, held, done = refs[:count], refs[count : 2 * count], refs[2 * count : -1], refs[-1]
    first = [
        pltpu.make_async_copy(sources[index], held[index], done.at[0, index])
        for index in range(count)
    ]
    second = [
        pltpu.make_async_copy(held[index], results[index], done.at[1, index])
        for index in range(count)
    ]
    for copy in first:
        copy.start()
    for copy, onward in zip(first, second):
        copy.wait()
        onward.start()
    for copy in second:
        copy.wait()


def per_device(
    feats,
    positions,
    species,
    wave_vectors,
    smearing,
    species_gain,
    w_charge,
    w_message,
    w_radial,
    w_out,
    edge_sender,
    edge_receiver,
    edge_mask,
    edge_length,
    ghost_down,
    ghost_up,
    cotangent,
):
    domains = lax.axis_size("dom")
    cells = lax.axis_size("cell")
    atoms, width = feats.shape[1:]
    ghosts = ghost_down.shape[1]
    bases = w_radial.shape[0]
    wave_count = wave_vectors.shape[1]
    devices = domains * cells
    chips = domains // 2
    f32, bf16 = jnp.float32, jnp.bfloat16
    vmem = pl.BlockSpec(memory_space=pltpu.VMEM)
    count = 3 * width + part_rows
    scratch = [
        pltpu.VMEM((domains, coord_rows, atoms), f32),
        pltpu.VMEM((domains, atoms, width), bf16),
        pltpu.VMEM((domains, atoms, width), bf16),
        pltpu.VMEM((2, ghosts, width), bf16),
        pltpu.VMEM((atoms + 2 * ghosts, width), bf16),
        pltpu.VMEM((2, ghosts, width), f32),
        pltpu.VMEM((2, ghosts, width), f32),
        pltpu.VMEM((bases * atoms, atoms + 2 * ghosts), f32),
        pltpu.VMEM((bases * atoms, atoms + 2 * ghosts), bf16),
        pltpu.VMEM((wave_count // 2, width), f32),
        pltpu.VMEM((wave_count, width), f32),
        pltpu.VMEM((coord_rows, wave_count // 2), f32),
        pltpu.VMEM((wave_count // 2, 3 * coord_rows), bf16),
        pltpu.VMEM((wave_count, domains * atoms), bf16),
        pltpu.VMEM((2 * atoms, wave_count), bf16),
        pltpu.VMEM((wave_count, width), bf16),
        pltpu.VMEM((2, 2, atoms, width), f32),
        pltpu.VMEM((2, atoms, width), f32),
        pltpu.VMEM((count, width), bf16),
        pltpu.VMEM((devices, part_rows, width), bf16),
        pltpu.VMEM((count, width), bf16),
        pltpu.VMEM((part_rows, width), bf16),
        pltpu.SemaphoreType.DMA((3, chips)),
        pltpu.SemaphoreType.DMA((3, chips)),
        pltpu.SemaphoreType.DMA((3, chips)),
        pltpu.SemaphoreType.DMA((3, chips)),
        pltpu.SemaphoreType.DMA((4,)),
        pltpu.SemaphoreType.DMA((4,)),
        pltpu.SemaphoreType.DMA((2,)),
        pltpu.SemaphoreType.DMA((2,)),
        pltpu.SemaphoreType.DMA((2,)),
        pltpu.SemaphoreType.DMA((2,)),
    ]
    shape = jax.ShapeDtypeStruct
    operands = (
        feats,
        positions.transpose(1, 0, 2),
        species,
        wave_vectors,
        smearing[None, :],
        species_gain,
        w_charge,
        w_message,
        w_radial,
        w_out,
        edge_sender,
        edge_receiver,
        edge_mask,
        edge_length,
        ghost_down,
        ghost_up,
        cotangent,
    )
    count = len(operands)
    staged = [pltpu.VMEM(value.shape, value.dtype) for value in operands]
    scratch = [*staged, *scratch, pltpu.SemaphoreType.DMA((count,))]
    outs = (
        shape(feats.shape, bf16),
        shape(feats.shape, bf16),
        shape((width, width), f32),
        shape((width, width), f32),
        shape((bases, width), f32),
        shape((width, width), f32),
    )

    def body(*refs):
        sources, rest = refs[:count], refs[count:]
        results, rest = rest[: len(outs)], rest[len(outs) :]
        block_kernel(domains, cells, sources, rest[:count], *results, *rest[count:])

    results = pl.pallas_call(
        body,
        out_shape=outs,
        in_specs=[pl.BlockSpec(memory_space=pltpu.HBM)] * count,
        out_specs=(vmem,) * len(outs),
        scratch_shapes=scratch,
        compiler_params=pltpu.CompilerParams(
            collective_id=0, has_side_effects=True, vmem_limit_bytes=64 * 1024 * 1024
        ),
        name="ewald_block",
    )(*operands)
    return pl.pallas_call(
        write_kernel,
        out_shape=outs,
        in_specs=[pl.BlockSpec(memory_space=pltpu.HBM)] * len(outs),
        out_specs=(pl.BlockSpec(memory_space=pltpu.HBM),) * len(outs),
        scratch_shapes=[
            *[pltpu.VMEM(out.shape, out.dtype) for out in outs],
            pltpu.SemaphoreType.DMA((2, len(outs))),
        ],
        compiler_params=pltpu.CompilerParams(vmem_limit_bytes=64 * 1024 * 1024),
        name="write_out",
    )(*results)


def solution(mesh):
    placed = (
        P("cell", "dom", None),
        P("cell", None, "dom"),
        P("cell", "dom"),
        P(),
        P(),
        P(),
        P(),
        P(),
        P(),
        P(),
        P("cell", "dom"),
        P("cell", "dom"),
        P("cell", "dom"),
        P("cell", "dom"),
        P("cell", "dom"),
        P("cell", "dom"),
        P("cell", "dom", None),
    )
    return jax.shard_map(
        per_device,
        mesh=mesh,
        in_specs=placed,
        out_specs=(P("cell", "dom", None), P("cell", "dom", None), P(), P(), P(), P()),
        check_vma=False,
    )
```
